32 devices in a mesh: parts: 2 (over y), dof: 1, mode: 8 (over z, x), sub: 2 (over core).
Axes of the slice: x: 2, y: 2, z: 4, core: 2. Of those that a mesh axis runs over, the one named last changes fastest.
Arguments:
- modes: bfloat16 [8192, 1024], P(('dof', 'sub'), ('parts', 'mode')), parts along dimension 1, may hold values from -6 to 6
- gyroscopic: bfloat16 [4, 32, 16, 128, 128], P(('parts', 'dof', 'sub'), 'mode'), parts along dimension 0, may hold values from -0.125 to 0.125
- centrifugal: bfloat16 [4, 32, 16, 128, 128], P(('parts', 'dof', 'sub'), 'mode'), parts along dimension 0, may hold values from -0.125 to 0.125
- pattern: int32 [2, 32, 16], P(('dof', 'sub'), 'mode'), may hold values from 0 to 63, as said below
Outputs:
- projected: float32 [4, 512, 512], P('parts', ('dof', 'sub'), 'mode'), parts along dimension 0
The draws below stay inside these ranges and needn't reach their ends.
There are 2 independent parts, one for each index of `parts`. The reference program is written for one: setup_inputs(seed, part) draws one part's arguments, and reference() takes and returns one part's arrays. A program takes and returns all parts, laid end to end along the dimension named above; an argument that names none is the same for every part. Nothing has to cross between parts.
Inputs may be any that keep to these rules, and one draw needn't show every extreme that they name: `pattern`: block row r names 16 distinct block columns (r + o) mod 64 with -8 <= o <= 8; o = 0 is among them, and so is o = 8 or o = -8.
All inputs are finite; a program needn't handle non-finite values.
Results may differ from the reference program's by a relative error of at most 0.0029.
Values may be sent and summed in bfloat16 or wider, within the bound.
No kernel may reach another device: no remote copies, remote signals or barrier semaphores. Data moves between devices by JAX's collectives and lax.ppermute only.
A program may use at most 64 MiB of HBM per device.

```python
import math
import jax
import jax.numpy as jnp
from jax import lax

M = 512
B = 128
NNZ = 16
HB = 8
U = 32
UNITS = 2
NBT = 64
NDOF = 8192


def draw_pattern(key, part):
    key = jax.random.fold_in(key, 7)
    skipped = jax.random.randint(key, (NBT,), 0, 2 * HB)
    skipped = skipped + (skipped >= HB).astype(jnp.int32)
    slot_index = jnp.arange(NNZ, dtype=jnp.int32)[None, :]
    picked = slot_index + (slot_index >= skipped[:, None]).astype(jnp.int32)
    offsets = picked - HB
    row_index = jnp.arange(NBT, dtype=jnp.int32)[:, None]
    columns = jnp.mod(row_index + offsets, NBT).astype(jnp.int32)
    return columns.reshape(UNITS, U, NNZ)


def strengthened(array, stream_key, source, target, shards_of, factor):
    owner, partner = [(jnp.arange(array.shape[axis_at]) // (array.shape[axis_at] // shards_of)).reshape([-1 if axis == axis_at else 1 for axis in range(array.ndim)]) for axis_at in (source, target)]
    chosen = jax.random.permutation(stream_key, shards_of)[partner]
    strong = (owner == chosen) | (owner == (partner + shards_of // 2) % shards_of)
    return jnp.where(strong, factor * array, array)


def level_of(rng, dims, pieces, low, largest):
    factor_of = 1.0
    for axis_at, parts in pieces:
        draws = jax.random.uniform(jax.random.fold_in(jax.random.fold_in(rng, 6), axis_at), (parts,), jnp.float32, low / len(pieces), largest / len(pieces))
        factor_of = factor_of * jnp.repeat(jnp.exp(draws), dims[axis_at] // parts).reshape((-1,) + (1,) * (len(dims) - 1 - axis_at))
    return factor_of


def scatter_about(stream_key, extent, deviation, reach, cuts=(), kind=jnp.bfloat16):
    level = level_of(stream_key, extent, cuts, -0.22, 0.18) if cuts else 1.0
    result = jax.random.normal(stream_key, extent, jnp.float32) * deviation * level
    return jnp.minimum(jnp.maximum(result, -reach), reach).astype(kind)


def noise_with(own_key, dims, deviation, most, split, heavy, kind=jnp.bfloat16):
    drawn = deviation * jax.random.normal(own_key, dims, jnp.float32)
    if split:
        drawn = drawn * level_of(own_key, dims, split, -0.22, 0.18)
    return jnp.clip(strengthened(drawn, jax.random.fold_in(own_key, 3), *heavy), -most, most).astype(kind)


def setup_inputs(seed: int = 0, part: int = 0) -> dict:
    seeds = jax.random.split(jax.random.key(seed), 5)
    own_keys = jax.random.split(jax.random.fold_in(seeds[4], part), 5)
    return {
        "modes": noise_with(own_keys[0], (NDOF, M), 1.0, 6.0, ((0, 2), (1, 8)), (0, 1, 8, 2.0)),
        "gyroscopic": scatter_about(own_keys[1], (UNITS, U, NNZ, B, B), (NNZ * B) ** -0.5, 0.125, ((0, 2), (1, 8))),
        "centrifugal": scatter_about(own_keys[2], (UNITS, U, NNZ, B, B), (NNZ * B) ** -0.5, 0.125, ((0, 2), (1, 8))),
        "pattern": draw_pattern(jax.random.fold_in(seeds[4], 71), part),
    }


def reference(modes, gyroscopic, centrifugal, pattern):
    unit_count = pattern.shape[0]
    per_unit = pattern.shape[1]
    block_total = unit_count * per_unit
    block_size = gyroscopic.shape[3]
    mode_width = modes.shape[1]
    mode_blocks = modes.reshape(block_total, block_size, mode_width)

    def accumulate(running, unit_index):
        gyro_part = lax.dynamic_index_in_dim(gyroscopic, unit_index, 0, keepdims=False).astype(jnp.float32)
        spin_part = lax.dynamic_index_in_dim(centrifugal, unit_index, 0, keepdims=False).astype(jnp.float32)
        slots = lax.dynamic_index_in_dim(pattern, unit_index, 0, keepdims=False).astype(jnp.int32)
        nearby = jnp.take(mode_blocks, slots, axis=0).astype(jnp.float32)
        gyro_image = jnp.einsum('jkab,jkbn->jan', gyro_part, nearby).astype(jnp.bfloat16)
        spin_image = jnp.einsum('jkab,jkbn->jan', spin_part, nearby).astype(jnp.bfloat16)
        own_rows = lax.dynamic_slice_in_dim(mode_blocks, (unit_index * per_unit).astype(jnp.int32), per_unit, 0)
        own_rows = own_rows.reshape(per_unit * block_size, mode_width).astype(jnp.float32)
        images = jnp.stack((gyro_image, spin_image)).reshape(2, per_unit * block_size, mode_width).astype(jnp.float32)
        running = running + jnp.einsum('rm,xrn->xmn', own_rows, images)
        return (running, None)
    start_sum = jnp.zeros((2, mode_width, mode_width), jnp.float32)
    running, _ = lax.scan(accumulate, start_sum, jnp.arange(unit_count, dtype=jnp.int32))
    return running * (1.0 / math.sqrt(block_total * block_size))
```

```python
import functools
import math

import jax
import jax.numpy as jnp
from jax import lax
from jax.experimental import pallas as pl
from jax.experimental.pallas import tpu as pltpu
from jax.sharding import PartitionSpec as P

HB = 8
X = 2
VMEM_LIMIT = 48 * 1024 * 1024
NT = (((1,), (1,)), ((), ()))


def ring(count):
    forward = [(i, (i + 1) % count) for i in range(count)]
    return forward, [(target, source) for source, target in forward]


def band_kernel(place, gyro, spin, band):
    row = pl.program_id(0)
    slots = gyro.shape[2]
    band[...] = jnp.zeros_like(band)
    for slot in range(slots):
        column = pl.multiple_of(place[row, slot] * 128, 128)
        band[0, 0, :, pl.ds(column, 128)] = gyro[0, 0, slot]
        band[1, 0, :, pl.ds(column, 128)] = spin[0, 0, slot]


def make_band(place, gyroscopic, centrifugal, width):
    _, rows, slots, size, _ = gyroscopic.shape
    block = pl.BlockSpec((1, 1, slots, size, size), lambda j, place: (0, j, 0, 0, 0))
    band = pl.pallas_call(
        band_kernel,
        out_shape=jax.ShapeDtypeStruct((2, rows, size, width), jnp.bfloat16),
        grid_spec=pltpu.PrefetchScalarGridSpec(
            num_scalar_prefetch=1,
            grid=(rows,),
            in_specs=[block, block],
            out_specs=pl.BlockSpec((2, 1, size, width), lambda j, place: (0, j, 0, 0)),
        ),
        compiler_params=pltpu.CompilerParams(vmem_limit_bytes=VMEM_LIMIT),
        name="band",
    )(place, gyroscopic, centrifugal)
    return band.reshape(2 * rows * size, width)


def image_kernel(group, info, own, cross, band, image, centre, lhs):
    offset = pl.multiple_of(info[0] * group, group)
    own_x = info[1]
    width = cross.shape[0]
    lhs[:width, :] = own[:, pl.ds(offset, cross.shape[1])]
    lhs[width:, :] = cross[...]
    image[...] = lax.dot_general(
        lhs[...], band[...], NT, preferred_element_type=jnp.float32
    ).astype(jnp.bfloat16)
    middle = pl.ds(2 * group, group)
    centre[pl.ds(pl.multiple_of(own_x * width, width), width), :] = lhs[:width, middle]
    centre[pl.ds(pl.multiple_of((1 - own_x) * width, width), width), :] = lhs[width:, middle]


def make_image(info, own, cross, band, group):
    width, span = cross.shape
    vmem = pl.BlockSpec(memory_space=pltpu.VMEM)
    return pl.pallas_call(
        functools.partial(image_kernel, group),
        out_shape=(
            jax.ShapeDtypeStruct((2 * width, band.shape[0]), jnp.bfloat16),
            jax.ShapeDtypeStruct((2 * width, group), jnp.bfloat16),
        ),
        in_specs=[pl.BlockSpec(memory_space=pltpu.SMEM), vmem, vmem, vmem],
        out_specs=(vmem, vmem),
        scratch_shapes=[pltpu.VMEM((2 * width, span), jnp.bfloat16)],
        compiler_params=pltpu.CompilerParams(vmem_limit_bytes=VMEM_LIMIT),
        cost_estimate=pl.CostEstimate(
            flops=4 * width * span * band.shape[0],
            bytes_accessed=2 * span * band.shape[0],
            transcendentals=0,
        ),
        name="image",
    )(info, own, cross, band)


def project_kernel(scaling, rows_out, info, *refs):
    images, centres = refs[:4], refs[4:8]
    keep, send, own_rows, stacked = refs[8:]
    pair = centres[0].shape[0]
    total, depth = own_rows.shape
    half = total // 2
    chunk = min(rows_out, pair)
    sub = info[8]
    for slot in range(4):
        start = info[slot] * pair
        for piece in range(pair // chunk):
            first = start + piece * chunk
            target = (
                lax.rem(lax.div(first, rows_out), 2) * half
                + lax.div(first, 2 * rows_out) * rows_out
                + lax.rem(first, rows_out)
            )
            own_rows[pl.ds(pl.multiple_of(target, chunk), chunk), :] = centres[slot][
                piece * chunk : (piece + 1) * chunk, :
            ]
        stacked[pl.ds(pl.multiple_of(info[4 + slot] * pair, pair), pair), :] = images[slot][...]
    mine = pl.ds(pl.multiple_of(sub * half, half), half)
    other = pl.ds(pl.multiple_of((1 - sub) * half, half), half)
    for matrix in range(2):
        part = stacked[:, matrix * depth : (matrix + 1) * depth]
        send[matrix] = (
            lax.dot_general(part, own_rows[other, :], NT, preferred_element_type=jnp.float32)
            * scaling
        ).astype(send.dtype)
        keep[matrix] = (
            lax.dot_general(part, own_rows[mine, :], NT, preferred_element_type=jnp.float32)
            * scaling
        )


def make_projection(info, images, centres, scaling, rows_out):
    pair, depth = centres[0].shape
    total = 4 * pair
    vmem = pl.BlockSpec(memory_space=pltpu.VMEM)
    return pl.pallas_call(
        functools.partial(project_kernel, scaling, rows_out),
        out_shape=(
            jax.ShapeDtypeStruct((2, total, total // 2), jnp.float32),
            jax.ShapeDtypeStruct((2, total, total // 2), jnp.bfloat16),
        ),
        in_specs=[pl.BlockSpec(memory_space=pltpu.SMEM)] + [vmem] * 8,
        out_specs=(vmem, vmem),
        scratch_shapes=[
            pltpu.VMEM((total, depth), jnp.bfloat16),
            pltpu.VMEM((total, images[0].shape[1]), jnp.bfloat16),
        ],
        compiler_params=pltpu.CompilerParams(vmem_limit_bytes=VMEM_LIMIT),
        cost_estimate=pl.CostEstimate(
            flops=4 * total * total * depth, bytes_accessed=4 * total * total, transcendentals=0
        ),
        name="project",
    )(info, *images, *centres)


def body(modes, gyroscopic, centrifugal, pattern):
    mode_count = lax.axis_size("mode")
    dof_count = lax.axis_size("dof")
    sub_count = lax.axis_size("sub")
    unit_count = dof_count * sub_count
    rows_dev = gyroscopic.shape[1]
    block_size = gyroscopic.shape[3]
    per_unit = rows_dev * mode_count
    block_total = unit_count * per_unit
    group = rows_dev * block_size
    total = modes.shape[1] * mode_count
    unit = lax.axis_index(("dof", "sub"))
    sub = lax.axis_index("sub")
    m = lax.axis_index("mode")
    z, x = m // X, m % X
    is_mid = (z == 1) | (z == 2)

    place = jnp.mod(pattern[0] - (unit * per_unit + m * rows_dev) + HB, block_total)
    band = make_band(place, gyroscopic, centrifugal, (rows_dev + 2 * HB) * block_size)

    phi = modes.T
    forward, backward = ring(unit_count)
    rim = HB * block_size
    low = lax.ppermute(phi[:, phi.shape[1] - rim :], ("dof", "sub"), forward)
    high = lax.ppermute(phi[:, :rim], ("dof", "sub"), backward)
    ext = jnp.concatenate([low, phi, high], axis=1)

    def window(array, first, count):
        return lax.dynamic_slice_in_dim(array, first * group, count * group, 1)

    def over_z(array, pairs):
        return lax.ppermute(
            array, "mode", [(s * X + i, t * X + i) for s, t in pairs for i in range(X)]
        )

    def over_x(array):
        return lax.ppermute(array, "mode", [(i, i ^ 1) for i in range(mode_count)])

    near = over_z(window(ext, 2 * (z ^ 1), 6), [(0, 1), (1, 0), (2, 3), (3, 2)])
    inner = over_z(window(ext, jnp.where(z == 1, 4, 0), 8), [(1, 2), (2, 1)])
    cross0 = over_x(window(ext, m ^ 1, 5))
    skip = over_z(window(ext, jnp.where(z == 0, 4, 2), 6), [(0, 2), (3, 1)])
    far = over_z(window(ext, jnp.where(z == 0, 6, 0), 6), [(0, 3), (3, 0)])
    passed = over_z(window(inner, jnp.where(z == 2, 2, 0), 6), [(2, 3), (1, 0)])
    crossA = over_x(window(near, 1 - x, 5))
    slotB = jnp.where(is_mid, window(inner, jnp.where(z == 1, 2, 0), 6), passed)
    crossB = over_x(window(slotB, 1 - x, 5))
    slotC = jnp.where(is_mid, skip, far)
    crossC = over_x(window(slotC, 1 - x, 5))

    pieces = []
    for own, cross, first in ((ext, cross0, m), (near, crossA, x), (slotB, crossB, x), (slotC, crossC, x)):
        info = jnp.stack([first, x]).astype(jnp.int32)
        pieces.append(make_image(info, own, cross, band, group))

    order_b = jnp.where(is_mid, 3, 2)
    order_c = jnp.where(is_mid, 2, 3)
    zero = jnp.zeros_like(z)
    info = jnp.stack(
        [z, z ^ 1, z ^ order_b, z ^ order_c, zero, zero + 1, order_b, order_c, sub]
    ).astype(jnp.int32)
    scaling = 1.0 / math.sqrt(block_total * block_size)
    keep, send = make_projection(
        info, [p[0] for p in pieces], [p[1] for p in pieces], scaling, total // unit_count
    )
    got = lax.ppermute(send, "sub", [(0, 1), (1, 0)])
    chip = keep + got.astype(jnp.float32)
    width = modes.shape[1]
    result = chip[:, :width]
    for j in range(1, mode_count):
        message = chip[:, j * width : (j + 1) * width].astype(jnp.bfloat16)
        arrived = lax.ppermute(message, "mode", [(i, i ^ j) for i in range(mode_count)])
        result = result + arrived.astype(jnp.float32)
    if dof_count > 1:
        result = lax.psum_scatter(result, "dof", scatter_dimension=2, tiled=True)
    return result.transpose(0, 2, 1)


def solution(mesh):
    return jax.shard_map(
        body,
        mesh=mesh,
        in_specs=(
            P(("dof", "sub"), ("parts", "mode")),
            P(("parts", "dof", "sub"), "mode", None, None, None),
            P(("parts", "dof", "sub"), "mode", None, None, None),
            P(("dof", "sub"), "mode", None),
        ),
        out_specs=P("parts", ("dof", "sub"), "mode"),
        check_vma=False,
    )
```

```python
import functools
import math

import jax
import jax.numpy as jnp
from jax import lax
from jax.experimental import pallas as pl
from jax.experimental.pallas import tpu as pltpu
from jax.sharding import PartitionSpec as P

HB = 8
X = 2
VMEM_LIMIT = 24 * 1024 * 1024
NT = (((1,), (1,)), ((), ()))
VMEM = pl.BlockSpec(memory_space=pltpu.VMEM)
ANY = pl.BlockSpec(memory_space=pl.ANY)


def params():
    return pltpu.CompilerParams(vmem_limit_bytes=VMEM_LIMIT)


def ring(count):
    forward = [(i, (i + 1) % count) for i in range(count)]
    return forward, [(target, source) for source, target in forward]


def place_in_mode():
    m = lax.axis_index("mode")
    return m, lax.div(m, X), lax.rem(m, X)


def inside(z):
    return (z == 1) | (z == 2)


def aligned(index, size):
    return pl.multiple_of(index * size, size)


def band_kernel(per_unit, block_total, pattern, gyro, spin, _, band):
    row = pl.program_id(0)
    slots, size = gyro.shape[2:4]
    unit = lax.axis_index(("dof", "sub"))
    base = unit * per_unit + lax.axis_index("mode") * pl.num_programs(0) - HB
    band[...] = jnp.zeros_like(band)
    for slot in range(slots):
        column = lax.rem(pattern[0, row, slot] - base + block_total, block_total)
        where = pl.ds(aligned(column, size), size)
        band[0, 0, :, where] = gyro[0, 0, slot]
        band[1, 0, :, where] = spin[0, 0, slot]


def make_band(pattern, gyroscopic, centrifugal, after, width, per_unit, block_total):
    _, rows, slots, size, _ = gyroscopic.shape
    block = pl.BlockSpec((1, 1, slots, size, size), lambda j: (0, j, 0, 0, 0))
    band = pl.pallas_call(
        functools.partial(band_kernel, per_unit, block_total),
        out_shape=jax.ShapeDtypeStruct((2, rows, size, width), jnp.bfloat16),
        grid=(rows,),
        in_specs=[pl.BlockSpec(memory_space=pltpu.SMEM), block, block, ANY],
        out_specs=pl.BlockSpec((2, 1, size, width), lambda j: (0, j, 0, 0)),
        compiler_params=params(),
        cost_estimate=pl.CostEstimate(flops=0, bytes_accessed=2**23, transcendentals=0),
        name="band",
    )(pattern, gyroscopic, centrifugal, after)
    return band.reshape(2 * rows * size, width)


def first_kernel(group, phi, low, high, ext, inner, near, cross, own):
    m, z, _ = place_in_mode()
    rim = low.shape[1]
    ext[:, :rim] = low[...]
    ext[:, rim : rim + phi.shape[1]] = phi[...]
    ext[:, rim + phi.shape[1] :] = high[...]

    def cut(out, start):
        out[...] = ext[:, pl.ds(aligned(start, group), out.shape[1])]

    cut(inner, jnp.where(z == 1, 4, 0))
    cut(near, 2 * (z + 1 - 2 * lax.rem(z, 2)))
    cut(cross, m + 1 - 2 * lax.rem(m, 2))
    cut(own, m)


def second_kernel(group, ext, inner, near, _, passed, cross, own, skip, far):
    _, z, x = place_in_mode()

    def cut(out, source, start):
        out[...] = source[:, pl.ds(aligned(start, group), out.shape[1])]

    cut(passed, inner, jnp.where(z == 2, 2, 0))
    cut(skip, ext, jnp.where(z == 0, 4, 2))
    cut(far, ext, jnp.where(z == 0, 6, 0))
    cut(cross, near, 1 - x)
    cut(own, near, x)


def choose_kernel(group, shift, middle, corner, *refs):
    cross, own = refs[-2:]
    _, z, x = place_in_mode()

    def cut(source, start):
        cross[...] = source[:, pl.ds(aligned(start + 1 - x, group), cross.shape[1])]
        own[...] = source[:, pl.ds(aligned(start + x, group), own.shape[1])]

    @pl.when(inside(z))
    def _():
        cut(middle, jnp.where(z == 1, shift, 0))

    @pl.when(jnp.logical_not(inside(z)))
    def _():
        cut(corner, 0)


def cutting(kernel, widths, name, *operands, after=()):
    rows = operands[0].shape[0]
    return pl.pallas_call(
        kernel,
        out_shape=[jax.ShapeDtypeStruct((rows, w), jnp.bfloat16) for w in widths],
        in_specs=[VMEM] * len(operands) + [ANY] * len(after),
        out_specs=[VMEM] * len(widths),
        compiler_params=params(),
        name=name,
    )(*operands, *after)


def fill(lhs, centre, pieces, middle):
    width = pieces[0].shape[0]
    _, _, x = place_in_mode()
    for slot in range(len(pieces) // 2):
        for side in range(2):
            first = (2 * slot + side) * width
            piece = pieces[2 * slot + side]
            lhs[first : first + width, :] = piece[...]
            chip = lax.rem(x + side, 2)
            centre[slot, pl.ds(aligned(chip, width), width), :] = piece[:, middle]


def image_kernel(middle, *refs):
    pieces, (band, image, centre, lhs) = refs[:4], refs[4:]
    fill(lhs, centre, pieces, middle)
    image[...] = lax.dot_general(
        lhs[...], band[...], NT, preferred_element_type=jnp.float32
    ).astype(jnp.bfloat16)


def make_image(pieces, band, group):
    width, span = pieces[0].shape
    return pl.pallas_call(
        functools.partial(image_kernel, slice(2 * group, 3 * group)),
        out_shape=(
            jax.ShapeDtypeStruct((4 * width, band.shape[0]), jnp.bfloat16),
            jax.ShapeDtypeStruct((2, 2 * width, group), jnp.bfloat16),
        ),
        in_specs=[VMEM] * 5,
        out_specs=(VMEM, VMEM),
        scratch_shapes=[pltpu.VMEM((4 * width, span), jnp.bfloat16)],
        compiler_params=params(),
        cost_estimate=pl.CostEstimate(
            flops=8 * width * span * band.shape[0], bytes_accessed=2**22, transcendentals=0
        ),
        name="image",
    )(*pieces, band)


def project_kernel(middle, scaling, rows_out, *refs):
    pieces, (band, image, centre) = refs[:4], refs[4:7]
    keep, send, own_rows, stacked, late, lhs = refs[7:]
    _, z, _ = place_in_mode()
    pair = centre.shape[1]
    total, depth = own_rows.shape
    half = total // 2
    chunk = min(rows_out, pair)
    fill(lhs, late, pieces, middle)
    late_image = lax.dot_general(
        lhs[...], band[...], NT, preferred_element_type=jnp.float32
    ).astype(jnp.bfloat16)
    near = z + 1 - 2 * lax.rem(z, 2)
    third = jnp.where(inside(z), 3 - z, lax.rem(z + 2, 4))
    last = jnp.where(inside(z), lax.rem(z + 2, 4), 3 - z)
    third_at = jnp.where(inside(z), 3, 2)
    stacked[: 2 * pair, :] = image[...]
    stacked[pl.ds(aligned(third_at, pair), pair), :] = late_image[:pair]
    stacked[pl.ds(aligned(5 - third_at, pair), pair), :] = late_image[pair:]
    for slot, chip_row in enumerate((z, near, third, last)):
        source = (centre, late)[slot // 2]
        for piece in range(pair // chunk):
            first = chip_row * pair + piece * chunk
            target = (
                lax.rem(lax.div(first, rows_out), 2) * half
                + lax.div(first, 2 * rows_out) * rows_out
                + lax.rem(first, rows_out)
            )
            own_rows[pl.ds(pl.multiple_of(target, chunk), chunk), :] = source[
                slot % 2, piece * chunk : (piece + 1) * chunk, :
            ]
    sub = lax.axis_index("sub")
    for matrix in range(2):
        part = stacked[:, matrix * depth : (matrix + 1) * depth]
        for out, side in ((send, 1 - sub), (keep, sub)):
            out[matrix] = (
                lax.dot_general(
                    part,
                    own_rows[pl.ds(aligned(side, half), half), :],
                    NT,
                    preferred_element_type=jnp.float32,
                )
                * scaling
            )


def make_projection(pieces, band, image, centre, group, scaling, rows_out):
    width, span = pieces[0].shape
    total = 8 * width
    part = jax.ShapeDtypeStruct((2, total, total // 2), jnp.float32)
    return pl.pallas_call(
        functools.partial(
            project_kernel, slice(2 * group, 3 * group), scaling, rows_out
        ),
        out_shape=(part, part),
        in_specs=[VMEM] * 7,
        out_specs=(VMEM, VMEM),
        scratch_shapes=[
            pltpu.VMEM((total, group), jnp.bfloat16),
            pltpu.VMEM((total, image.shape[1]), jnp.bfloat16),
            pltpu.VMEM(centre.shape, jnp.bfloat16),
            pltpu.VMEM((4 * width, span), jnp.bfloat16),
        ],
        compiler_params=params(),
        cost_estimate=pl.CostEstimate(
            flops=4 * total * total * group, bytes_accessed=2**22, transcendentals=0
        ),
        name="project",
    )(*pieces, band, image, centre)


def body(modes, gyroscopic, centrifugal, pattern):
    mode_count = lax.axis_size("mode")
    dof_count = lax.axis_size("dof")
    sub_count = lax.axis_size("sub")
    unit_count = dof_count * sub_count
    rows_dev = gyroscopic.shape[1]
    block_size = gyroscopic.shape[3]
    per_unit = rows_dev * mode_count
    block_total = unit_count * per_unit
    group = rows_dev * block_size
    width = modes.shape[1]
    total = width * mode_count

    def over_z(array, pairs):
        return lax.ppermute(
            array, "mode", [(s * X + i, t * X + i) for s, t in pairs for i in range(X)]
        )

    def over_x(array):
        return lax.ppermute(array, "mode", [(i, i ^ 1) for i in range(mode_count)])

    phi = modes.T
    forward, backward = ring(unit_count)
    rim = HB * block_size
    low = lax.ppermute(phi[:, phi.shape[1] - rim :], ("dof", "sub"), forward)
    high = lax.ppermute(phi[:, :rim], ("dof", "sub"), backward)

    w5, w6, w8 = 5 * group, 6 * group, 8 * group
    ext, inner_w, near_w, cross0_w, own0 = cutting(
        functools.partial(first_kernel, group),
        (phi.shape[1] + 2 * rim, w8, w6, w5, w5),
        "first",
        phi,
        low,
        high,
    )
    inner = over_z(inner_w, [(1, 2), (2, 1)])
    near = over_z(near_w, [(0, 1), (1, 0), (2, 3), (3, 2)])
    cross0 = over_x(cross0_w)
    band = make_band(pattern, gyroscopic, centrifugal, own0, w5, per_unit, block_total)

    passed_w, crossA_w, ownA, skip_w, far_w = cutting(
        functools.partial(second_kernel, group),
        (w6, w5, w5, w6, w6),
        "second",
        ext,
        inner,
        near,
        after=(band,),
    )
    passed = over_z(passed_w, [(2, 3), (1, 0)])
    skip = over_z(skip_w, [(0, 2), (3, 1)])
    far = over_z(far_w, [(0, 3), (3, 0)])
    crossA = over_x(crossA_w)
    image, centre = make_image((own0, cross0, ownA, crossA), band, group)

    crossB_w, ownB = cutting(
        functools.partial(choose_kernel, group, 2), (w5, w5), "third", inner, passed
    )
    crossB = over_x(crossB_w)
    crossC_w, ownC = cutting(
        functools.partial(choose_kernel, group, 0), (w5, w5), "fourth", skip, far, after=(image,)
    )
    crossC = over_x(crossC_w)

    scaling = 1.0 / math.sqrt(block_total * block_size)
    keep, send = make_projection(
        (ownB, crossB, ownC, crossC), band, image, centre, group, scaling, total // unit_count
    )
    got = lax.ppermute(send, "sub", [(0, 1), (1, 0)])
    chip = keep + got
    result = chip[:, :width]
    for j in range(mode_count - 1, 0, -1):
        message = chip[:, j * width : (j + 1) * width].astype(jnp.bfloat16)
        arrived = lax.ppermute(message, "mode", [(i, i ^ j) for i in range(mode_count)])
        result = result + arrived.astype(jnp.float32)
    if dof_count > 1:
        result = lax.psum_scatter(result, "dof", scatter_dimension=2, tiled=True)
    return result.transpose(0, 2, 1)


def solution(mesh):
    return jax.shard_map(
        body,
        mesh=mesh,
        in_specs=(
            P(("dof", "sub"), ("parts", "mode")),
            P(("parts", "dof", "sub"), "mode", None, None, None),
            P(("parts", "dof", "sub"), "mode", None, None, None),
            P(("dof", "sub"), "mode", None),
        ),
        out_specs=P("parts", ("dof", "sub"), "mode"),
        check_vma=False,
    )
```

```python
import functools
import math

import jax
import jax.numpy as jnp
from jax import lax
from jax.experimental import pallas as pl
from jax.experimental.pallas import tpu as pltpu
from jax.sharding import PartitionSpec as P

HB = 8
X = 2
VMEM_LIMIT = 24 * 1024 * 1024
NT = (((1,), (1,)), ((), ()))
VMEM = pl.BlockSpec(memory_space=pltpu.VMEM)
ANY = pl.BlockSpec(memory_space=pl.ANY)


def params():
    return pltpu.CompilerParams(vmem_limit_bytes=VMEM_LIMIT)


def ring(count):
    forward = [(i, (i + 1) % count) for i in range(count)]
    return forward, [(target, source) for source, target in forward]


def place_in_mode():
    m = lax.axis_index("mode")
    return m, lax.div(m, X), lax.rem(m, X)


def inside(z):
    return (z == 1) | (z == 2)


def aligned(index, size):
    return pl.multiple_of(index * size, size)


def band_kernel(per_unit, block_total, pattern, gyro, spin, _, band):
    row = pl.program_id(0)
    slots, size = gyro.shape[2:4]
    unit = lax.axis_index(("dof", "sub"))
    base = unit * per_unit + lax.axis_index("mode") * pl.num_programs(0) - HB
    band[...] = jnp.zeros_like(band)
    for slot in range(slots):
        column = lax.rem(pattern[0, row, slot] - base + block_total, block_total)
        where = pl.ds(aligned(column, size), size)
        band[0, 0, :, where] = gyro[0, 0, slot]
        band[1, 0, :, where] = spin[0, 0, slot]


def make_band(pattern, gyroscopic, centrifugal, after, width, per_unit, block_total):
    _, rows, slots, size, _ = gyroscopic.shape
    block = pl.BlockSpec((1, 1, slots, size, size), lambda j: (0, j, 0, 0, 0))
    band = pl.pallas_call(
        functools.partial(band_kernel, per_unit, block_total),
        out_shape=jax.ShapeDtypeStruct((2, rows, size, width), jnp.bfloat16),
        grid=(rows,),
        in_specs=[pl.BlockSpec(memory_space=pltpu.SMEM), block, block, ANY],
        out_specs=pl.BlockSpec((2, 1, size, width), lambda j: (0, j, 0, 0)),
        compiler_params=params(),
        cost_estimate=pl.CostEstimate(flops=0, bytes_accessed=2**23, transcendentals=0),
        name="band",
    )(pattern, gyroscopic, centrifugal, after)
    return band.reshape(2 * rows * size, width)


def rim_kernel(phi, low, high):
    low[...] = phi[:, phi.shape[1] - low.shape[1] :]
    high[...] = phi[:, : high.shape[1]]


def cut(group, out, source, start):
    out[...] = source[:, pl.ds(aligned(start, group), out.shape[1])]


def first_kernel(group, phi, low, high, ext, inner, far, near, cross, own):
    m, z, _ = place_in_mode()
    rim = low.shape[1]
    ext[:, :rim] = low[...]
    ext[:, rim : rim + phi.shape[1]] = phi[...]
    ext[:, rim + phi.shape[1] :] = high[...]
    cut(group, inner, ext, jnp.where(z == 1, 4, 0))
    cut(group, far, ext, jnp.where(z == 0, 6, 0))
    cut(group, near, ext, 2 * (z + 1 - 2 * lax.rem(z, 2)))
    cut(group, cross, ext, m + 1 - 2 * lax.rem(m, 2))
    cut(group, own, ext, m)


def near_kernel(group, near, cross, own):
    _, _, x = place_in_mode()
    cut(group, cross, near, 1 - x)
    cut(group, own, near, x)


def middle_kernel(group, ext, inner, far, _, passed, skip, cross, own):
    _, z, x = place_in_mode()
    cut(group, passed, inner, jnp.where(z == 2, 2, 0))
    cut(group, skip, ext, jnp.where(z == 0, 4, 2))

    @pl.when(inside(z))
    def _():
        first = jnp.where(z == 1, 2, 0)
        cut(group, cross, inner, first + 1 - x)
        cut(group, own, inner, first + x)

    @pl.when(jnp.logical_not(inside(z)))
    def _():
        cut(group, cross, far, 1 - x)
        cut(group, own, far, x)


def last_kernel(group, skip, passed, _, cross, own):
    _, z, x = place_in_mode()

    @pl.when(inside(z))
    def _():
        cut(group, cross, skip, 1 - x)
        cut(group, own, skip, x)

    @pl.when(jnp.logical_not(inside(z)))
    def _():
        cut(group, cross, passed, 1 - x)
        cut(group, own, passed, x)


def cutting(kernel, widths, name, *operands, after=()):
    rows = operands[0].shape[0]
    return pl.pallas_call(
        kernel,
        out_shape=[jax.ShapeDtypeStruct((rows, w), jnp.bfloat16) for w in widths],
        in_specs=[VMEM] * len(operands) + [ANY] * len(after),
        out_specs=[VMEM] * len(widths),
        compiler_params=params(),
        name=name,
    )(*operands, *after)


def fill(lhs, centre, pieces, middle):
    width = pieces[0].shape[0]
    _, _, x = place_in_mode()
    for slot in range(len(pieces) // 2):
        for side in range(2):
            first = (2 * slot + side) * width
            piece = pieces[2 * slot + side]
            lhs[first : first + width, :] = piece[...]
            chip = lax.rem(x + side, 2)
            centre[slot, pl.ds(aligned(chip, width), width), :] = piece[:, middle]


def image_kernel(middle, *refs):
    pieces, (band, image, centre, lhs) = refs[:4], refs[4:]
    fill(lhs, centre, pieces, middle)
    image[...] = lax.dot_general(
        lhs[...], band[...], NT, preferred_element_type=jnp.float32
    ).astype(jnp.bfloat16)


def make_image(pieces, band, group):
    width, span = pieces[0].shape
    return pl.pallas_call(
        functools.partial(image_kernel, slice(2 * group, 3 * group)),
        out_shape=(
            jax.ShapeDtypeStruct((4 * width, band.shape[0]), jnp.bfloat16),
            jax.ShapeDtypeStruct((2, 2 * width, group), jnp.bfloat16),
        ),
        in_specs=[VMEM] * 5,
        out_specs=(VMEM, VMEM),
        scratch_shapes=[pltpu.VMEM((4 * width, span), jnp.bfloat16)],
        compiler_params=params(),
        cost_estimate=pl.CostEstimate(
            flops=8 * width * span * band.shape[0], bytes_accessed=2**22, transcendentals=0
        ),
        name="image",
    )(*pieces, band)


def project_kernel(matrix, middle, scaling, rows_out, *refs):
    pieces, (band, image, centre) = refs[:4], refs[4:7]
    keep, send, own_rows, stacked, late, lhs = refs[7:]
    _, z, _ = place_in_mode()
    pair = centre.shape[1]
    total, depth = own_rows.shape
    half = total // 2
    chunk = min(rows_out, pair)
    columns = slice(matrix * depth, (matrix + 1) * depth)
    fill(lhs, late, pieces, middle)
    late_image = lax.dot_general(
        lhs[...], band[columns, :], NT, preferred_element_type=jnp.float32
    ).astype(jnp.bfloat16)
    stacked[: 2 * pair, :] = image[:, columns]
    stacked[2 * pair : 3 * pair, :] = late_image[pair:]
    stacked[3 * pair :, :] = late_image[:pair]
    near = z + 1 - 2 * lax.rem(z, 2)
    for slot, chip_row in enumerate((z, near, 3 - z, lax.rem(z + 2, 4))):
        source = (centre, late)[slot // 2]
        for piece in range(pair // chunk):
            first = chip_row * pair + piece * chunk
            target = (
                lax.rem(lax.div(first, rows_out), 2) * half
                + lax.div(first, 2 * rows_out) * rows_out
                + lax.rem(first, rows_out)
            )
            own_rows[pl.ds(pl.multiple_of(target, chunk), chunk), :] = source[
                slot % 2, piece * chunk : (piece + 1) * chunk, :
            ]
    sub = lax.axis_index("sub")
    for out, side in ((send, 1 - sub), (keep, sub)):
        out[...] = (
            lax.dot_general(
                stacked[...],
                own_rows[pl.ds(aligned(side, half), half), :],
                NT,
                preferred_element_type=jnp.float32,
            )
            * scaling
        )


def make_projection(matrix, pieces, band, image, centre, group, scaling, rows_out):
    width, span = pieces[0].shape
    total = 8 * width
    part = jax.ShapeDtypeStruct((total, total // 2), jnp.float32)
    return pl.pallas_call(
        functools.partial(
            project_kernel, matrix, slice(2 * group, 3 * group), scaling, rows_out
        ),
        out_shape=(part, part),
        in_specs=[VMEM] * 7,
        out_specs=(VMEM, VMEM),
        scratch_shapes=[
            pltpu.VMEM((total, group), jnp.bfloat16),
            pltpu.VMEM((total, group), jnp.bfloat16),
            pltpu.VMEM(centre.shape, jnp.bfloat16),
            pltpu.VMEM((4 * width, span), jnp.bfloat16),
        ],
        compiler_params=params(),
        cost_estimate=pl.CostEstimate(
            flops=2 * total * total * group, bytes_accessed=2**21, transcendentals=0
        ),
        name="project",
    )(*pieces, band, image, centre)


def body(modes, gyroscopic, centrifugal, pattern):
    mode_count = lax.axis_size("mode")
    dof_count = lax.axis_size("dof")
    sub_count = lax.axis_size("sub")
    unit_count = dof_count * sub_count
    rows_dev = gyroscopic.shape[1]
    block_size = gyroscopic.shape[3]
    per_unit = rows_dev * mode_count
    block_total = unit_count * per_unit
    group = rows_dev * block_size
    width = modes.shape[1]
    total = width * mode_count

    def over_z(array, pairs):
        return lax.ppermute(
            array, "mode", [(s * X + i, t * X + i) for s, t in pairs for i in range(X)]
        )

    def over_x(array):
        return lax.ppermute(array, "mode", [(i, i ^ 1) for i in range(mode_count)])

    phi = modes.T
    forward, backward = ring(unit_count)
    rim = HB * block_size
    low_w, high_w = cutting(rim_kernel, (rim, rim), "rims", phi)
    low = lax.ppermute(low_w, ("dof", "sub"), forward)
    high = lax.ppermute(high_w, ("dof", "sub"), backward)

    w5, w6, w8 = 5 * group, 6 * group, 8 * group
    ext, inner_w, far_w, near_w, cross0_w, own0 = cutting(
        functools.partial(first_kernel, group),
        (phi.shape[1] + 2 * rim, w8, w6, w6, w5, w5),
        "first",
        phi,
        low,
        high,
    )
    inner = over_z(inner_w, [(1, 2), (2, 1)])
    far = over_z(far_w, [(0, 3), (3, 0)])
    near = over_z(near_w, [(0, 1), (1, 0), (2, 3), (3, 2)])
    cross0 = over_x(cross0_w)
    band = make_band(pattern, gyroscopic, centrifugal, own0, w5, per_unit, block_total)

    crossA_w, ownA = cutting(functools.partial(near_kernel, group), (w5, w5), "near", near)
    crossA = over_x(crossA_w)
    passed_w, skip_w, crossB_w, ownB = cutting(
        functools.partial(middle_kernel, group),
        (w6, w6, w5, w5),
        "middle",
        ext,
        inner,
        far,
        after=(band,),
    )
    passed = over_z(passed_w, [(2, 3), (1, 0)])
    skip = over_z(skip_w, [(0, 2), (3, 1)])
    crossB = over_x(crossB_w)
    image, centre = make_image((own0, cross0, ownA, crossA), band, group)
    crossC_w, ownC = cutting(
        functools.partial(last_kernel, group), (w5, w5), "last", skip, passed, after=(image,)
    )
    crossC = over_x(crossC_w)

    scaling = 1.0 / math.sqrt(block_total * block_size)
    sums = []
    for matrix in range(2):
        keep, send = make_projection(
            matrix,
            (ownB, crossB, ownC, crossC),
            band,
            image,
            centre,
            group,
            scaling,
            total // unit_count,
        )
        sums.append(keep + lax.ppermute(send, "sub", [(0, 1), (1, 0)]))
    chip = jnp.stack(sums)
    result = chip[:, :width]
    for j in range(mode_count - 1, 0, -1):
        message = chip[:, j * width : (j + 1) * width].astype(jnp.bfloat16)
        arrived = lax.ppermute(message, "mode", [(i, i ^ j) for i in range(mode_count)])
        result = result + arrived.astype(jnp.float32)
    if dof_count > 1:
        result = lax.psum_scatter(result, "dof", scatter_dimension=2, tiled=True)
    return result.transpose(0, 2, 1)


def solution(mesh):
    return jax.shard_map(
        body,
        mesh=mesh,
        in_specs=(
            P(("dof", "sub"), ("parts", "mode")),
            P(("parts", "dof", "sub"), "mode", None, None, None),
            P(("parts", "dof", "sub"), "mode", None, None, None),
            P(("dof", "sub"), "mode", None),
        ),
        out_specs=P("parts", ("dof", "sub"), "mode"),
        check_vma=False,
    )
```

```python
import functools
import math

import jax
import jax.numpy as jnp
from jax import lax
from jax.experimental import pallas as pl
from jax.experimental.pallas import tpu as pltpu
from jax.sharding import PartitionSpec as P

HB = 8
X = 2
EARLY = 48
VMEM_LIMIT = 24 * 1024 * 1024
NT = (((1,), (1,)), ((), ()))
VMEM = pl.BlockSpec(memory_space=pltpu.VMEM)
ANY = pl.BlockSpec(memory_space=pl.ANY)


def params():
    return pltpu.CompilerParams(vmem_limit_bytes=VMEM_LIMIT)


def ring(count):
    forward = [(i, (i + 1) % count) for i in range(count)]
    return forward, [(target, source) for source, target in forward]


def place_in_mode():
    m = lax.axis_index("mode")
    return m, lax.div(m, X), lax.rem(m, X)


def ahead(z):
    return lax.rem(3 * (z + 1), 5) - 1


def behind(z):
    return lax.rem(2 * (z + 1), 5) - 1


def aligned(index, size):
    return pl.multiple_of(index * size, size)


def band_kernel(per_unit, block_total, pattern, gyro, spin, _, band):
    row = pl.program_id(0)
    slots, size = gyro.shape[2:4]
    unit = lax.axis_index(("dof", "sub"))
    base = unit * per_unit + lax.axis_index("mode") * pl.num_programs(0) - HB
    band[...] = jnp.zeros_like(band)
    for slot in range(slots):
        column = lax.rem(pattern[0, row, slot] - base + block_total, block_total)
        where = pl.ds(aligned(column, size), size)
        band[0, 0, :, where] = gyro[0, 0, slot]
        band[1, 0, :, where] = spin[0, 0, slot]


def make_band(pattern, gyroscopic, centrifugal, after, width, per_unit, block_total):
    _, rows, slots, size, _ = gyroscopic.shape
    block = pl.BlockSpec((1, 1, slots, size, size), lambda j: (0, j, 0, 0, 0))
    band = pl.pallas_call(
        functools.partial(band_kernel, per_unit, block_total),
        out_shape=jax.ShapeDtypeStruct((2, rows, size, width), jnp.bfloat16),
        grid=(rows,),
        in_specs=[pl.BlockSpec(memory_space=pltpu.SMEM), block, block, ANY],
        out_specs=pl.BlockSpec((2, 1, size, width), lambda j: (0, j, 0, 0)),
        compiler_params=params(),
        cost_estimate=pl.CostEstimate(flops=0, bytes_accessed=2**23, transcendentals=0),
        name="band",
    )(pattern, gyroscopic, centrifugal, after)
    return band.reshape(2 * rows * size, width)


def rim_kernel(phi, low, high):
    low[...] = phi[:, phi.shape[1] - low.shape[1] :]
    high[...] = phi[:, : high.shape[1]]


def cut(group, out, source, start):
    out[...] = source[:, pl.ds(aligned(start, group), out.shape[1])]


def first_kernel(group, phi, low, high, ext, to_ahead, to_behind, cross, own):
    m, z, _ = place_in_mode()
    rim = low.shape[1]
    ext[:, :rim] = low[...]
    ext[:, rim : rim + phi.shape[1]] = phi[...]
    ext[:, rim + phi.shape[1] :] = high[...]
    cut(group, to_ahead, ext, 2 * ahead(z))
    cut(group, to_behind, ext, 2 * behind(z))
    cut(group, cross, ext, m + 1 - 2 * lax.rem(m, 2))
    cut(group, own, ext, m)


def parted_kernel(group, got, *refs):
    cross, own = refs[-2:]
    _, _, x = place_in_mode()
    cut(group, cross, got, 1 - x)
    cut(group, own, got, x)


def onward_kernel(group, rows, got, ext, *refs):
    cross, own, out = refs[-3:]
    _, z, x = place_in_mode()
    cut(group, cross, got, 1 - x)
    cut(group, own, got, x)
    out[...] = ext[rows, pl.ds(aligned(2 * (3 - z), group), out.shape[1])]


def cutting(kernel, shapes, name, *operands, after=()):
    return pl.pallas_call(
        kernel,
        out_shape=[jax.ShapeDtypeStruct(shape, jnp.bfloat16) for shape in shapes],
        in_specs=[VMEM] * len(operands) + [ANY] * len(after),
        out_specs=[VMEM] * len(shapes),
        compiler_params=params(),
        name=name,
    )(*operands, *after)


def fill(lhs, centre, slots, middle):
    _, _, x = place_in_mode()
    width = centre.shape[1] // 2
    for slot, sides in enumerate(slots):
        for side, chunks in enumerate(sides):
            chip = aligned(lax.rem(x + side, 2), width)
            at = 0
            for chunk in chunks:
                first = (2 * slot + side) * width + at
                count = chunk.shape[0]
                lhs[first : first + count, :] = chunk[...]
                centre[slot, pl.ds(pl.multiple_of(chip + at, 16), count), :] = chunk[:, middle]
                at += count


def regroup(layout, refs):
    refs = iter(refs)
    return [[[next(refs) for _ in range(chunks)] for _ in range(2)] for chunks in layout]


def image_kernel(layout, middle, *refs):
    band, image, centre, lhs = refs[-4:]
    fill(lhs, centre, regroup(layout, refs[:-4]), middle)
    image[...] = lax.dot_general(
        lhs[...], band[...], NT, preferred_element_type=jnp.float32
    ).astype(jnp.bfloat16)


def flat(slots):
    layout = [len(sides[0]) for sides in slots]
    return layout, [chunk for sides in slots for chunks in sides for chunk in chunks]


def make_image(slots, band, group, width):
    layout, pieces = flat(slots)
    span = pieces[0].shape[1]
    return pl.pallas_call(
        functools.partial(image_kernel, layout, slice(2 * group, 3 * group)),
        out_shape=(
            jax.ShapeDtypeStruct((4 * width, band.shape[0]), jnp.bfloat16),
            jax.ShapeDtypeStruct((2, 2 * width, group), jnp.bfloat16),
        ),
        in_specs=[VMEM] * (len(pieces) + 1),
        out_specs=(VMEM, VMEM),
        scratch_shapes=[pltpu.VMEM((4 * width, span), jnp.bfloat16)],
        compiler_params=params(),
        cost_estimate=pl.CostEstimate(
            flops=8 * width * span * band.shape[0], bytes_accessed=2**22, transcendentals=0
        ),
        name="image",
    )(*pieces, band)


def project_kernel(matrix, layout, middle, scaling, rows_out, *refs):
    keep, send, own_rows, stacked, late, lhs = refs[-6:]
    band, image, centre = refs[-9:-6]
    _, z, _ = place_in_mode()
    pair = centre.shape[1]
    total, depth = own_rows.shape
    half = total // 2
    chunk = min(rows_out, pair)
    columns = slice(matrix * depth, (matrix + 1) * depth)
    fill(lhs, late, regroup(layout, refs[:-9]), middle)
    stacked[: 2 * pair, :] = image[:, columns]
    stacked[2 * pair :, :] = lax.dot_general(
        lhs[...], band[columns, :], NT, preferred_element_type=jnp.float32
    ).astype(jnp.bfloat16)
    for slot, chip_row in enumerate((z, behind(z), ahead(z), 3 - z)):
        source = (centre, late)[slot // 2]
        for piece in range(pair // chunk):
            first = chip_row * pair + piece * chunk
            target = (
                lax.rem(lax.div(first, rows_out), 2) * half
                + lax.div(first, 2 * rows_out) * rows_out
                + lax.rem(first, rows_out)
            )
            own_rows[pl.ds(pl.multiple_of(target, chunk), chunk), :] = source[
                slot % 2, piece * chunk : (piece + 1) * chunk, :
            ]
    sub = lax.axis_index("sub")
    for out, side in ((send, 1 - sub), (keep, sub)):
        out[...] = (
            lax.dot_general(
                stacked[...],
                own_rows[pl.ds(aligned(side, half), half), :],
                NT,
                preferred_element_type=jnp.float32,
            )
            * scaling
        )


def make_projection(matrix, slots, band, image, centre, group, scaling, rows_out):
    layout, pieces = flat(slots)
    total = 2 * image.shape[0]
    part = jax.ShapeDtypeStruct((total, total // 2), jnp.float32)
    return pl.pallas_call(
        functools.partial(
            project_kernel, matrix, layout, slice(2 * group, 3 * group), scaling, rows_out
        ),
        out_shape=(part, part),
        in_specs=[VMEM] * (len(pieces) + 3),
        out_specs=(VMEM, VMEM),
        scratch_shapes=[
            pltpu.VMEM((total, group), jnp.bfloat16),
            pltpu.VMEM((total, group), jnp.bfloat16),
            pltpu.VMEM(centre.shape, jnp.bfloat16),
            pltpu.VMEM((total // 2, pieces[0].shape[1]), jnp.bfloat16),
        ],
        compiler_params=params(),
        cost_estimate=pl.CostEstimate(
            flops=2 * total * total * group, bytes_accessed=2**21, transcendentals=0
        ),
        name="project",
    )(*pieces, band, image, centre)


def body(modes, gyroscopic, centrifugal, pattern):
    mode_count = lax.axis_size("mode")
    dof_count = lax.axis_size("dof")
    sub_count = lax.axis_size("sub")
    unit_count = dof_count * sub_count
    rows_dev = gyroscopic.shape[1]
    block_size = gyroscopic.shape[3]
    per_unit = rows_dev * mode_count
    block_total = unit_count * per_unit
    group = rows_dev * block_size
    width = modes.shape[1]
    total = width * mode_count

    def move(array, to):
        target, flip = to
        pairs = [(i, target(i // X) * X + (i % X ^ flip)) for i in range(mode_count)]
        return lax.ppermute(array, "mode", pairs)

    def to_ahead(z):
        return 3 * (z + 1) % 5 - 1

    def to_behind(z):
        return 2 * (z + 1) % 5 - 1

    def to_far(z):
        return 3 - z

    def to_same(z):
        return z

    phi = modes.T
    forward, backward = ring(unit_count)
    rim = HB * block_size
    low_w, high_w = cutting(rim_kernel, [(width, rim)] * 2, "rims", phi)
    low = lax.ppermute(low_w, ("dof", "sub"), forward)
    high = lax.ppermute(high_w, ("dof", "sub"), backward)

    w5, w6 = 5 * group, 6 * group
    ext, ahead_w, behind_w, cross0_w, own0 = cutting(
        functools.partial(first_kernel, group),
        [(width, w) for w in (phi.shape[1] + 2 * rim, w6, w6, w5, w5)],
        "first",
        phi,
        low,
        high,
    )
    gotA = move(ahead_w, (to_ahead, 0))
    gotB = move(behind_w, (to_behind, 0))
    cross0 = move(cross0_w, (to_same, 1))
    band = make_band(pattern, gyroscopic, centrifugal, own0, w5, per_unit, block_total)

    early = EARLY
    crossA_w, ownA, far1_w = cutting(
        functools.partial(onward_kernel, group, slice(0, early)),
        [(width, w5), (width, w5), (early, w6)],
        "onward",
        gotA,
        ext,
        after=(band,),
    )
    far1 = move(far1_w, (to_far, 0))
    crossA = move(crossA_w, (to_same, 1))
    crossB_w, ownB, far2_w = cutting(
        functools.partial(onward_kernel, group, slice(early, width)),
        [(width, w5), (width, w5), (width - early, w6)],
        "onward",
        gotB,
        ext,
        after=(crossA_w,),
    )
    far2 = move(far2_w, (to_far, 0))
    crossB = move(crossB_w, (to_same, 1))
    image, centre = make_image(
        [([own0], [cross0]), ([ownA], [crossA])], band, group, width
    )
    crossC1_w, ownC1 = cutting(
        functools.partial(parted_kernel, group), [(early, w5)] * 2, "parted", far1, after=(image,)
    )
    crossC1 = move(crossC1_w, (to_same, 1))
    crossC2_w, ownC2 = cutting(
        functools.partial(parted_kernel, group), [(width - early, w5)] * 2, "parted", far2
    )
    crossC2 = move(crossC2_w, (to_same, 1))

    scaling = 1.0 / math.sqrt(block_total * block_size)
    sums = []
    for matrix in range(2):
        keep, send = make_projection(
            matrix,
            [([ownB], [crossB]), ([ownC1, ownC2], [crossC1, crossC2])],
            band,
            image,
            centre,
            group,
            scaling,
            total // unit_count,
        )
        sums.append(keep + lax.ppermute(send, "sub", [(0, 1), (1, 0)]))
    chip = jnp.stack(sums)
    result = chip[:, :width]
    for slot, to in ((3, to_far), (2, to_ahead), (1, to_behind), (0, to_same)):
        for flip in range(X):
            if slot == 0 and flip == 0:
                continue
            first = (slot * X + flip) * width
            message = chip[:, first : first + width].astype(jnp.bfloat16)
            result = result + move(message, (to, flip)).astype(jnp.float32)
    if dof_count > 1:
        result = lax.psum_scatter(result, "dof", scatter_dimension=2, tiled=True)
    return result.transpose(0, 2, 1)


def solution(mesh):
    return jax.shard_map(
        body,
        mesh=mesh,
        in_specs=(
            P(("dof", "sub"), ("parts", "mode")),
            P(("parts", "dof", "sub"), "mode", None, None, None),
            P(("parts", "dof", "sub"), "mode", None, None, None),
            P(("dof", "sub"), "mode", None),
        ),
        out_specs=P("parts", ("dof", "sub"), "mode"),
        check_vma=False,
    )
```

```python
import functools
import math

import jax
import jax.numpy as jnp
from jax import lax
from jax.experimental import pallas as pl
from jax.experimental.pallas import tpu as pltpu
from jax.sharding import PartitionSpec as P

HB = 8
X = 2
PIECES = (32, 32)
VMEM_LIMIT = 24 * 1024 * 1024
NT = (((1,), (1,)), ((), ()))
VMEM = pl.BlockSpec(memory_space=pltpu.VMEM)
ANY = pl.BlockSpec(memory_space=pl.ANY)


def params():
    return pltpu.CompilerParams(vmem_limit_bytes=VMEM_LIMIT)


def ring(count):
    forward = [(i, (i + 1) % count) for i in range(count)]
    return forward, [(target, source) for source, target in forward]


def place_in_mode():
    m = lax.axis_index("mode")
    return m, lax.div(m, X), lax.rem(m, X)


def ahead(z):
    return lax.rem(3 * (z + 1), 5) - 1


def behind(z):
    return lax.rem(2 * (z + 1), 5) - 1


def aligned(index, size):
    return pl.multiple_of(index * size, size)


def band_kernel(per_unit, block_total, pattern, gyro, spin, _, band):
    row = pl.program_id(0)
    slots, size = gyro.shape[2:4]
    unit = lax.axis_index(("dof", "sub"))
    base = unit * per_unit + lax.axis_index("mode") * pl.num_programs(0) - HB
    band[...] = jnp.zeros_like(band)
    for slot in range(slots):
        column = lax.rem(pattern[0, row, slot] - base + block_total, block_total)
        where = pl.ds(aligned(column, size), size)
        band[0, 0, :, where] = gyro[0, 0, slot]
        band[1, 0, :, where] = spin[0, 0, slot]


def make_band(pattern, gyroscopic, centrifugal, after, width, per_unit, block_total):
    _, rows, slots, size, _ = gyroscopic.shape
    block = pl.BlockSpec((1, 1, slots, size, size), lambda j: (0, j, 0, 0, 0))
    band = pl.pallas_call(
        functools.partial(band_kernel, per_unit, block_total),
        out_shape=jax.ShapeDtypeStruct((2, rows, size, width), jnp.bfloat16),
        grid=(rows,),
        in_specs=[pl.BlockSpec(memory_space=pltpu.SMEM), block, block, ANY],
        out_specs=pl.BlockSpec((2, 1, size, width), lambda j: (0, j, 0, 0)),
        compiler_params=params(),
        cost_estimate=pl.CostEstimate(flops=0, bytes_accessed=2**23, transcendentals=0),
        name="band",
    )(pattern, gyroscopic, centrifugal, after)
    return band.reshape(2 * rows * size, width)


def cut(group, out, source, start):
    out[...] = source[:, pl.ds(aligned(start, group), out.shape[1])]


def stage_kernel(phi, out):
    pltpu.sync_copy(phi, out)


def stage(phi):
    return pl.pallas_call(
        stage_kernel,
        out_shape=jax.ShapeDtypeStruct(phi.shape, phi.dtype),
        in_specs=[ANY],
        out_specs=VMEM,
        compiler_params=params(),
        name="stage",
    )(phi)


def first_kernel(group, rim, phi, below, above, ext, to_ahead, to_behind, cross, own):
    m, z, _ = place_in_mode()
    ext[:, :rim] = below[:, below.shape[1] - rim :]
    ext[:, rim : rim + phi.shape[1]] = phi[...]
    ext[:, rim + phi.shape[1] :] = above[:, :rim]
    cut(group, to_ahead, ext, 2 * ahead(z))
    cut(group, to_behind, ext, 2 * behind(z))
    cut(group, cross, ext, m + 1 - 2 * lax.rem(m, 2))
    cut(group, own, ext, m)


def parted_kernel(group, got, *refs):
    cross, own = refs[-2:]
    _, _, x = place_in_mode()
    cut(group, cross, got, 1 - x)
    cut(group, own, got, x)


def onward_kernel(group, got, ext, *refs):
    cross, own, *far = refs[-2 - len(PIECES) :]
    _, z, x = place_in_mode()
    cut(group, cross, got, 1 - x)
    cut(group, own, got, x)
    at = 0
    for out in far:
        rows, span = out.shape
        out[...] = ext[at : at + rows, pl.ds(aligned(2 * (3 - z), group), span)]
        at += rows


def cutting(kernel, shapes, name, *operands, after=()):
    return pl.pallas_call(
        kernel,
        out_shape=[jax.ShapeDtypeStruct(shape, jnp.bfloat16) for shape in shapes],
        in_specs=[VMEM] * len(operands) + [ANY] * len(after),
        out_specs=[VMEM] * len(shapes),
        compiler_params=params(),
        name=name,
    )(*operands, *after)


def fill(lhs, centre, slots, middle):
    _, _, x = place_in_mode()
    width = centre.shape[1] // 2
    for slot, sides in enumerate(slots):
        for side, chunks in enumerate(sides):
            chip = aligned(lax.rem(x + side, 2), width)
            at = 0
            for chunk in chunks:
                first = (2 * slot + side) * width + at
                count = chunk.shape[0]
                lhs[first : first + count, :] = chunk[...]
                centre[slot, pl.ds(pl.multiple_of(chip + at, 16), count), :] = chunk[:, middle]
                at += count


def regroup(layout, refs):
    refs = iter(refs)
    return [[[next(refs) for _ in range(chunks)] for _ in range(2)] for chunks in layout]


def image_kernel(layout, middle, *refs):
    band, image, centre, lhs = refs[-4:]
    fill(lhs, centre, regroup(layout, refs[:-4]), middle)
    image[...] = lax.dot_general(
        lhs[...], band[...], NT, preferred_element_type=jnp.float32
    ).astype(jnp.bfloat16)


def flat(slots):
    layout = [len(sides[0]) for sides in slots]
    return layout, [chunk for sides in slots for chunks in sides for chunk in chunks]


def make_image(slots, band, group, width):
    layout, pieces = flat(slots)
    span = pieces[0].shape[1]
    return pl.pallas_call(
        functools.partial(image_kernel, layout, slice(2 * group, 3 * group)),
        out_shape=(
            jax.ShapeDtypeStruct((4 * width, band.shape[0]), jnp.bfloat16),
            jax.ShapeDtypeStruct((2, 2 * width, group), jnp.bfloat16),
        ),
        in_specs=[VMEM] * (len(pieces) + 1),
        out_specs=(VMEM, VMEM),
        scratch_shapes=[pltpu.VMEM((4 * width, span), jnp.bfloat16)],
        compiler_params=params(),
        cost_estimate=pl.CostEstimate(
            flops=8 * width * span * band.shape[0], bytes_accessed=2**22, transcendentals=0
        ),
        name="image",
    )(*pieces, band)


def project_kernel(matrix, layout, middle, scaling, rows_out, *refs):
    keep, send, own_rows, stacked, late, lhs = refs[-6:]
    band, image, centre = refs[-9:-6]
    _, z, _ = place_in_mode()
    pair = centre.shape[1]
    total, depth = own_rows.shape
    half = total // 2
    chunk = min(rows_out, pair)
    columns = slice(matrix * depth, (matrix + 1) * depth)
    fill(lhs, late, regroup(layout, refs[:-9]), middle)
    stacked[: 2 * pair, :] = image[:, columns]
    stacked[2 * pair :, :] = lax.dot_general(
        lhs[...], band[columns, :], NT, preferred_element_type=jnp.float32
    ).astype(jnp.bfloat16)
    for slot, chip_row in enumerate((z, behind(z), ahead(z), 3 - z)):
        source = (centre, late)[slot // 2]
        for piece in range(pair // chunk):
            first = chip_row * pair + piece * chunk
            target = (
                lax.rem(lax.div(first, rows_out), 2) * half
                + lax.div(first, 2 * rows_out) * rows_out
                + lax.rem(first, rows_out)
            )
            own_rows[pl.ds(pl.multiple_of(target, chunk), chunk), :] = source[
                slot % 2, piece * chunk : (piece + 1) * chunk, :
            ]
    sub = lax.axis_index("sub")
    for out, side in ((send, 1 - sub), (keep, sub)):
        out[...] = (
            lax.dot_general(
                stacked[...],
                own_rows[pl.ds(aligned(side, half), half), :],
                NT,
                preferred_element_type=jnp.float32,
            )
            * scaling
        )


def make_projection(matrix, slots, band, image, centre, group, scaling, rows_out):
    layout, pieces = flat(slots)
    total = 2 * image.shape[0]
    part = jax.ShapeDtypeStruct((total, total // 2), jnp.float32)
    return pl.pallas_call(
        functools.partial(
            project_kernel, matrix, layout, slice(2 * group, 3 * group), scaling, rows_out
        ),
        out_shape=(part, part),
        in_specs=[VMEM] * (len(pieces) + 3),
        out_specs=(VMEM, VMEM),
        scratch_shapes=[
            pltpu.VMEM((total, group), jnp.bfloat16),
            pltpu.VMEM((total, group), jnp.bfloat16),
            pltpu.VMEM(centre.shape, jnp.bfloat16),
            pltpu.VMEM((total // 2, pieces[0].shape[1]), jnp.bfloat16),
        ],
        compiler_params=params(),
        cost_estimate=pl.CostEstimate(
            flops=2 * total * total * group, bytes_accessed=2**21, transcendentals=0
        ),
        name="project",
    )(*pieces, band, image, centre)


def body(modes, gyroscopic, centrifugal, pattern):
    mode_count = lax.axis_size("mode")
    dof_count = lax.axis_size("dof")
    sub_count = lax.axis_size("sub")
    unit_count = dof_count * sub_count
    rows_dev = gyroscopic.shape[1]
    block_size = gyroscopic.shape[3]
    per_unit = rows_dev * mode_count
    block_total = unit_count * per_unit
    group = rows_dev * block_size
    width = modes.shape[1]
    total = width * mode_count

    def move(array, to):
        target, flip = to
        pairs = [(i, target(i // X) * X + (i % X ^ flip)) for i in range(mode_count)]
        return lax.ppermute(array, "mode", pairs)

    def to_ahead(z):
        return 3 * (z + 1) % 5 - 1

    def to_behind(z):
        return 2 * (z + 1) % 5 - 1

    def to_far(z):
        return 3 - z

    def to_same(z):
        return z

    phi = modes.T
    forward, backward = ring(unit_count)
    rim = HB * block_size
    units = ("dof", "sub")
    if unit_count == 2:
        below = above = lax.ppermute(phi, units, forward)
    else:
        below = lax.ppermute(phi[:, phi.shape[1] - rim :], units, forward)
        above = lax.ppermute(phi[:, :rim], units, backward)

    w5, w6 = 5 * group, 6 * group
    ext, ahead_w, behind_w, cross0_w, own0 = cutting(
        functools.partial(first_kernel, group, rim),
        [(width, w) for w in (phi.shape[1] + 2 * rim, w6, w6, w5, w5)],
        "first",
        stage(phi),
        below,
        above,
    )
    gotA = move(ahead_w, (to_ahead, 0))
    gotB = move(behind_w, (to_behind, 0))
    cross0 = move(cross0_w, (to_same, 1))
    band = make_band(pattern, gyroscopic, centrifugal, own0, w5, per_unit, block_total)

    crossA_w, ownA, *far_w = cutting(
        functools.partial(onward_kernel, group),
        [(width, w5), (width, w5)] + [(rows, w6) for rows in PIECES],
        "onward",
        gotA,
        ext,
        after=(band,),
    )
    far = [move(piece, (to_far, 0)) for piece in far_w]
    crossA = move(crossA_w, (to_same, 1))
    crossB_w, ownB = cutting(
        functools.partial(parted_kernel, group),
        [(width, w5), (width, w5)],
        "parted",
        gotB,
        after=(crossA_w,),
    )
    crossB = move(crossB_w, (to_same, 1))
    image, centre = make_image(
        [([own0], [cross0]), ([ownA], [crossA])], band, group, width
    )
    ownC, crossC = [], []
    for piece in far:
        cross_w, own = cutting(
            functools.partial(parted_kernel, group),
            [(piece.shape[0], w5)] * 2,
            "parted",
            piece,
            after=(image,),
        )
        ownC.append(own)
        crossC.append(move(cross_w, (to_same, 1)))

    scaling = 1.0 / math.sqrt(block_total * block_size)
    sums = []
    for matrix in range(2):
        keep, send = make_projection(
            matrix,
            [([ownB], [crossB]), (ownC, crossC)],
            band,
            image,
            centre,
            group,
            scaling,
            total // unit_count,
        )
        sums.append(keep + lax.ppermute(send, "sub", [(0, 1), (1, 0)]))
    chip = jnp.stack(sums)
    result = chip[:, :width]
    for slot, to in ((0, to_same), (1, to_behind), (2, to_ahead), (3, to_far)):
        for flip in range(X):
            if slot == 0 and flip == 0:
                continue
            first = (slot * X + flip) * width
            message = chip[:, first : first + width].astype(jnp.bfloat16)
            result = result + move(message, (to, flip)).astype(jnp.float32)
    if dof_count > 1:
        result = lax.psum_scatter(result, "dof", scatter_dimension=2, tiled=True)
    return result.transpose(0, 2, 1)


def solution(mesh):
    return jax.shard_map(
        body,
        mesh=mesh,
        in_specs=(
            P(("dof", "sub"), ("parts", "mode")),
            P(("parts", "dof", "sub"), "mode", None, None, None),
            P(("parts", "dof", "sub"), "mode", None, None, None),
            P(("dof", "sub"), "mode", None),
        ),
        out_specs=P("parts", ("dof", "sub"), "mode"),
        check_vma=False,
    )
```

```python
import functools
import math

import jax
import jax.numpy as jnp
from jax import lax
from jax.experimental import pallas as pl
from jax.experimental.pallas import tpu as pltpu
from jax.sharding import PartitionSpec as P

HB = 8
X = 2
PIECES = (32, 16, 16)
VMEM_LIMIT = 24 * 1024 * 1024
NT = (((1,), (1,)), ((), ()))
VMEM = pl.BlockSpec(memory_space=pltpu.VMEM)
ANY = pl.BlockSpec(memory_space=pl.ANY)


def params():
    return pltpu.CompilerParams(vmem_limit_bytes=VMEM_LIMIT)


def ring(count):
    forward = [(i, (i + 1) % count) for i in range(count)]
    return forward, [(target, source) for source, target in forward]


def place_in_mode():
    m = lax.axis_index("mode")
    return m, lax.div(m, X), lax.rem(m, X)


def ahead(z):
    return lax.rem(3 * (z + 1), 5) - 1


def behind(z):
    return lax.rem(2 * (z + 1), 5) - 1


def aligned(index, size):
    return pl.multiple_of(index * size, size)


def band_kernel(per_unit, block_total, pattern, gyro, spin, _, band):
    row = pl.program_id(0)
    slots, size = gyro.shape[2:4]
    unit = lax.axis_index(("dof", "sub"))
    base = unit * per_unit + lax.axis_index("mode") * pl.num_programs(0) - HB
    band[...] = jnp.zeros_like(band)
    for slot in range(slots):
        column = lax.rem(pattern[0, row, slot] - base + block_total, block_total)
        where = pl.ds(aligned(column, size), size)
        band[0, 0, :, where] = gyro[0, 0, slot]
        band[1, 0, :, where] = spin[0, 0, slot]


def make_band(pattern, gyroscopic, centrifugal, after, width, per_unit, block_total):
    _, rows, slots, size, _ = gyroscopic.shape
    block = pl.BlockSpec((1, 1, slots, size, size), lambda j: (0, j, 0, 0, 0))
    band = pl.pallas_call(
        functools.partial(band_kernel, per_unit, block_total),
        out_shape=jax.ShapeDtypeStruct((2, rows, size, width), jnp.bfloat16),
        grid=(rows,),
        in_specs=[pl.BlockSpec(memory_space=pltpu.SMEM), block, block, ANY],
        out_specs=pl.BlockSpec((2, 1, size, width), lambda j: (0, j, 0, 0)),
        compiler_params=params(),
        cost_estimate=pl.CostEstimate(flops=0, bytes_accessed=2**23, transcendentals=0),
        name="band",
    )(pattern, gyroscopic, centrifugal, after)
    return band.reshape(2 * rows * size, width)


def cut(group, out, source, start):
    out[...] = source[:, pl.ds(aligned(start, group), out.shape[1])]


def plain_start(z):
    return jnp.where(z < 2, 2 * z, 2 * z - 2)


def plain_kernel(group, phi, out):
    _, z, _ = place_in_mode()
    pltpu.sync_copy(phi.at[:, pl.ds(aligned(plain_start(ahead(z)), group), out.shape[1])], out)


def cut_plain(phi, group):
    return pl.pallas_call(
        functools.partial(plain_kernel, group),
        out_shape=jax.ShapeDtypeStruct((phi.shape[0], 4 * group), phi.dtype),
        in_specs=[ANY],
        out_specs=VMEM,
        compiler_params=params(),
        name="plain",
    )(phi)


def stage_kernel(phi, out):
    pltpu.sync_copy(phi, out)


def stage(phi):
    return pl.pallas_call(
        stage_kernel,
        out_shape=jax.ShapeDtypeStruct(phi.shape, phi.dtype),
        in_specs=[ANY],
        out_specs=VMEM,
        compiler_params=params(),
        name="stage",
    )(phi)


def first_kernel(group, rim, phi, below, above, ext, to_ahead, to_behind, cross, own):
    m, z, _ = place_in_mode()
    ext[:, :rim] = below[:, below.shape[1] - rim :]
    ext[:, rim : rim + phi.shape[1]] = phi[...]
    ext[:, rim + phi.shape[1] :] = above[:, :rim]
    target = ahead(z)
    cut(group, to_ahead, ext, jnp.where(target < 2, 2 * target, 2 * target + 4))
    cut(group, to_behind, ext, 2 * behind(z))
    cut(group, cross, ext, m + 1 - 2 * lax.rem(m, 2))
    cut(group, own, ext, m)


def parted_kernel(group, got, *refs):
    cross, own = refs[-2:]
    _, _, x = place_in_mode()
    cut(group, cross, got, 1 - x)
    cut(group, own, got, x)


def onward_kernel(group, plain, rim, ext, *refs):
    cross, own, *far = refs[-2 - len(PIECES) :]
    _, z, x = place_in_mode()

    def part(out, first):
        for lower, order in ((True, (rim, plain)), (False, (plain, rim))):
            for shift in range(2):

                @pl.when(((z < 2) == lower) & (first == shift))
                def _():
                    split = order[0].shape[1] - shift * group
                    out[:, :split] = order[0][:, shift * group :]
                    out[:, split:] = order[1][:, : out.shape[1] - split]

    part(cross, 1 - x)
    part(own, x)
    at = 0
    for out in far:
        rows, span = out.shape
        out[...] = ext[at : at + rows, pl.ds(aligned(2 * (3 - z), group), span)]
        at += rows


def cutting(kernel, shapes, name, *operands, after=()):
    return pl.pallas_call(
        kernel,
        out_shape=[jax.ShapeDtypeStruct(shape, jnp.bfloat16) for shape in shapes],
        in_specs=[VMEM] * len(operands) + [ANY] * len(after),
        out_specs=[VMEM] * len(shapes),
        compiler_params=params(),
        name=name,
    )(*operands, *after)


def fill(lhs, centre, slots, middle):
    _, _, x = place_in_mode()
    width = centre.shape[1] // 2
    for slot, sides in enumerate(slots):
        for side, chunks in enumerate(sides):
            chip = aligned(lax.rem(x + side, 2), width)
            at = 0
            for chunk in chunks:
                first = (2 * slot + side) * width + at
                count = chunk.shape[0]
                lhs[first : first + count, :] = chunk[...]
                centre[slot, pl.ds(pl.multiple_of(chip + at, 16), count), :] = chunk[:, middle]
                at += count


def regroup(layout, refs):
    refs = iter(refs)
    return [[[next(refs) for _ in range(chunks)] for _ in range(2)] for chunks in layout]


def image_kernel(layout, middle, *refs):
    band, image, centre, lhs = refs[-4:]
    fill(lhs, centre, regroup(layout, refs[:-4]), middle)
    image[...] = lax.dot_general(
        lhs[...], band[...], NT, preferred_element_type=jnp.float32
    ).astype(jnp.bfloat16)


def flat(slots):
    layout = [len(sides[0]) for sides in slots]
    return layout, [chunk for sides in slots for chunks in sides for chunk in chunks]


def make_image(slots, band, group, width):
    layout, pieces = flat(slots)
    span = pieces[0].shape[1]
    return pl.pallas_call(
        functools.partial(image_kernel, layout, slice(2 * group, 3 * group)),
        out_shape=(
            jax.ShapeDtypeStruct((4 * width, band.shape[0]), jnp.bfloat16),
            jax.ShapeDtypeStruct((2, 2 * width, group), jnp.bfloat16),
        ),
        in_specs=[VMEM] * (len(pieces) + 1),
        out_specs=(VMEM, VMEM),
        scratch_shapes=[pltpu.VMEM((4 * width, span), jnp.bfloat16)],
        compiler_params=params(),
        cost_estimate=pl.CostEstimate(
            flops=8 * width * span * band.shape[0], bytes_accessed=2**22, transcendentals=0
        ),
        name="image",
    )(*pieces, band)


def project_kernel(matrix, layout, middle, scaling, rows_out, *refs):
    keep, send, own_rows, stacked, late, lhs = refs[-6:]
    band, image, centre = refs[-9:-6]
    _, z, _ = place_in_mode()
    pair = centre.shape[1]
    total, depth = own_rows.shape
    half = total // 2
    chunk = min(rows_out, pair)
    columns = slice(matrix * depth, (matrix + 1) * depth)
    fill(lhs, late, regroup(layout, refs[:-9]), middle)
    stacked[: 2 * pair, :] = image[:, columns]
    stacked[2 * pair :, :] = lax.dot_general(
        lhs[...], band[columns, :], NT, preferred_element_type=jnp.float32
    ).astype(jnp.bfloat16)
    for slot, chip_row in enumerate((z, behind(z), ahead(z), 3 - z)):
        source = (centre, late)[slot // 2]
        for piece in range(pair // chunk):
            first = chip_row * pair + piece * chunk
            target = (
                lax.rem(lax.div(first, rows_out), 2) * half
                + lax.div(first, 2 * rows_out) * rows_out
                + lax.rem(first, rows_out)
            )
            own_rows[pl.ds(pl.multiple_of(target, chunk), chunk), :] = source[
                slot % 2, piece * chunk : (piece + 1) * chunk, :
            ]
    sub = lax.axis_index("sub")
    for out, side in ((send, 1 - sub), (keep, sub)):
        out[...] = (
            lax.dot_general(
                stacked[...],
                own_rows[pl.ds(aligned(side, half), half), :],
                NT,
                preferred_element_type=jnp.float32,
            )
            * scaling
        )


def make_projection(matrix, slots, band, image, centre, group, scaling, rows_out):
    layout, pieces = flat(slots)
    total = 2 * image.shape[0]
    part = jax.ShapeDtypeStruct((total, total // 2), jnp.float32)
    return pl.pallas_call(
        functools.partial(
            project_kernel, matrix, layout, slice(2 * group, 3 * group), scaling, rows_out
        ),
        out_shape=(part, part),
        in_specs=[VMEM] * (len(pieces) + 3),
        out_specs=(VMEM, VMEM),
        scratch_shapes=[
            pltpu.VMEM((total, group), jnp.bfloat16),
            pltpu.VMEM((total, group), jnp.bfloat16),
            pltpu.VMEM(centre.shape, jnp.bfloat16),
            pltpu.VMEM((total // 2, pieces[0].shape[1]), jnp.bfloat16),
        ],
        compiler_params=params(),
        cost_estimate=pl.CostEstimate(
            flops=2 * total * total * group, bytes_accessed=2**21, transcendentals=0
        ),
        name="project",
    )(*pieces, band, image, centre)


def body(modes, gyroscopic, centrifugal, pattern):
    mode_count = lax.axis_size("mode")
    dof_count = lax.axis_size("dof")
    sub_count = lax.axis_size("sub")
    unit_count = dof_count * sub_count
    rows_dev = gyroscopic.shape[1]
    block_size = gyroscopic.shape[3]
    per_unit = rows_dev * mode_count
    block_total = unit_count * per_unit
    group = rows_dev * block_size
    width = modes.shape[1]
    total = width * mode_count

    def move(array, to):
        target, flip = to
        pairs = [(i, target(i // X) * X + (i % X ^ flip)) for i in range(mode_count)]
        return lax.ppermute(array, "mode", pairs)

    def to_ahead(z):
        return 3 * (z + 1) % 5 - 1

    def to_behind(z):
        return 2 * (z + 1) % 5 - 1

    def to_far(z):
        return 3 - z

    def to_same(z):
        return z

    phi = modes.T
    forward, backward = ring(unit_count)
    rim = HB * block_size
    plainA = move(cut_plain(phi, group), (to_ahead, 0))
    units = ("dof", "sub")
    if unit_count == 2:
        below = above = lax.ppermute(phi, units, forward)
    else:
        below = lax.ppermute(phi[:, phi.shape[1] - rim :], units, forward)
        above = lax.ppermute(phi[:, :rim], units, backward)

    w5, w6 = 5 * group, 6 * group
    ext, ahead_w, behind_w, cross0_w, own0 = cutting(
        functools.partial(first_kernel, group, rim),
        [(width, w) for w in (phi.shape[1] + 2 * rim, 2 * group, w6, w5, w5)],
        "first",
        stage(phi),
        below,
        above,
    )
    gotA = move(ahead_w, (to_ahead, 0))
    gotB = move(behind_w, (to_behind, 0))
    cross0 = move(cross0_w, (to_same, 1))
    band = make_band(pattern, gyroscopic, centrifugal, own0, w5, per_unit, block_total)

    crossA_w, ownA, *far_w = cutting(
        functools.partial(onward_kernel, group),
        [(width, w5), (width, w5)] + [(rows, w6) for rows in PIECES],
        "onward",
        plainA,
        gotA,
        ext,
        after=(band,),
    )
    far = [move(piece, (to_far, 0)) for piece in far_w]
    crossA = move(crossA_w, (to_same, 1))
    crossB_w, ownB = cutting(
        functools.partial(parted_kernel, group),
        [(width, w5), (width, w5)],
        "parted",
        gotB,
        after=(crossA_w,),
    )
    crossB = move(crossB_w, (to_same, 1))
    image, centre = make_image(
        [([own0], [cross0]), ([ownA], [crossA])], band, group, width
    )
    ownC, crossC = [], []
    for piece in far:
        cross_w, own = cutting(
            functools.partial(parted_kernel, group),
            [(piece.shape[0], w5)] * 2,
            "parted",
            piece,
            after=(image,),
        )
        ownC.append(own)
        crossC.append(move(cross_w, (to_same, 1)))

    scaling = 1.0 / math.sqrt(block_total * block_size)
    sums = []
    for matrix in range(2):
        keep, send = make_projection(
            matrix,
            [([ownB], [crossB]), (ownC, crossC)],
            band,
            image,
            centre,
            group,
            scaling,
            total // unit_count,
        )
        sums.append(keep + lax.ppermute(send, "sub", [(0, 1), (1, 0)]))
    chip = jnp.stack(sums)
    result = chip[:, :width]
    for slot, to in ((0, to_same), (1, to_behind), (2, to_ahead), (3, to_far)):
        for flip in range(X):
            if slot == 0 and flip == 0:
                continue
            first = (slot * X + flip) * width
            message = chip[:, first : first + width].astype(jnp.bfloat16)
            result = result + move(message, (to, flip)).astype(jnp.float32)
    if dof_count > 1:
        result = lax.psum_scatter(result, "dof", scatter_dimension=2, tiled=True)
    return result.transpose(0, 2, 1)


def solution(mesh):
    return jax.shard_map(
        body,
        mesh=mesh,
        in_specs=(
            P(("dof", "sub"), ("parts", "mode")),
            P(("parts", "dof", "sub"), "mode", None, None, None),
            P(("parts", "dof", "sub"), "mode", None, None, None),
            P(("dof", "sub"), "mode", None),
        ),
        out_specs=P("parts", ("dof", "sub"), "mode"),
        check_vma=False,
    )
```

```python
import functools
import math

import jax
import jax.numpy as jnp
from jax import lax
from jax.experimental import pallas as pl
from jax.experimental.pallas import tpu as pltpu
from jax.sharding import PartitionSpec as P

HB = 8
X = 2
PIECES = (32, 32)
VMEM_LIMIT = 24 * 1024 * 1024
NT = (((1,), (1,)), ((), ()))
VMEM = pl.BlockSpec(memory_space=pltpu.VMEM)
ANY = pl.BlockSpec(memory_space=pl.ANY)


def params():
    return pltpu.CompilerParams(vmem_limit_bytes=VMEM_LIMIT)


def ring(count):
    forward = [(i, (i + 1) % count) for i in range(count)]
    return forward, [(target, source) for source, target in forward]


def place_in_mode():
    m = lax.axis_index("mode")
    return m, lax.div(m, X), lax.rem(m, X)


def ahead(z):
    return lax.rem(3 * (z + 1), 5) - 1


def behind(z):
    return lax.rem(2 * (z + 1), 5) - 1


def aligned(index, size):
    return pl.multiple_of(index * size, size)


def band_kernel(per_unit, block_total, pattern, gyro, spin, _, band):
    row = pl.program_id(0)
    slots, size = gyro.shape[2:4]
    unit = lax.axis_index(("dof", "sub"))
    base = unit * per_unit + lax.axis_index("mode") * pl.num_programs(0) - HB
    band[...] = jnp.zeros_like(band)
    for slot in range(slots):
        column = lax.rem(pattern[0, row, slot] - base + block_total, block_total)
        where = pl.ds(aligned(column, size), size)
        band[0, 0, :, where] = gyro[0, 0, slot]
        band[1, 0, :, where] = spin[0, 0, slot]


def make_band(pattern, gyroscopic, centrifugal, after, width, per_unit, block_total):
    _, rows, slots, size, _ = gyroscopic.shape
    block = pl.BlockSpec((1, 1, slots, size, size), lambda j: (0, j, 0, 0, 0))
    band = pl.pallas_call(
        functools.partial(band_kernel, per_unit, block_total),
        out_shape=jax.ShapeDtypeStruct((2, rows, size, width), jnp.bfloat16),
        grid=(rows,),
        in_specs=[pl.BlockSpec(memory_space=pltpu.SMEM), block, block, ANY],
        out_specs=pl.BlockSpec((2, 1, size, width), lambda j: (0, j, 0, 0)),
        compiler_params=params(),
        cost_estimate=pl.CostEstimate(flops=0, bytes_accessed=2**23, transcendentals=0),
        name="band",
    )(pattern, gyroscopic, centrifugal, after)
    return band.reshape(2 * rows * size, width)


def cut(group, out, source, start):
    out[...] = source[:, pl.ds(aligned(start, group), out.shape[1])]


def plain_start(z):
    return jnp.where(z < 2, 2 * z, 2 * z - 2)


def plain_kernel(group, phi, out):
    _, z, _ = place_in_mode()
    pltpu.sync_copy(phi.at[:, pl.ds(aligned(plain_start(ahead(z)), group), out.shape[1])], out)


def cut_plain(phi, group):
    return pl.pallas_call(
        functools.partial(plain_kernel, group),
        out_shape=jax.ShapeDtypeStruct((phi.shape[0], 4 * group), phi.dtype),
        in_specs=[ANY],
        out_specs=VMEM,
        compiler_params=params(),
        name="plain",
    )(phi)


def stage_kernel(phi, out):
    pltpu.sync_copy(phi, out)


def stage(phi):
    return pl.pallas_call(
        stage_kernel,
        out_shape=jax.ShapeDtypeStruct(phi.shape, phi.dtype),
        in_specs=[ANY],
        out_specs=VMEM,
        compiler_params=params(),
        name="stage",
    )(phi)


def first_kernel(group, rim, phi, below, above, ext, to_ahead, to_behind, cross, own):
    m, z, _ = place_in_mode()
    ext[:, :rim] = below[:, below.shape[1] - rim :]
    ext[:, rim : rim + phi.shape[1]] = phi[...]
    ext[:, rim + phi.shape[1] :] = above[:, :rim]
    target = ahead(z)
    cut(group, to_ahead, ext, jnp.where(target < 2, 2 * target, 2 * target + 4))
    cut(group, to_behind, ext, 2 * behind(z))
    cut(group, cross, ext, m + 1 - 2 * lax.rem(m, 2))
    cut(group, own, ext, m)


def parted_kernel(group, got, *refs):
    cross, own = refs[-2:]
    _, _, x = place_in_mode()
    cut(group, cross, got, 1 - x)
    cut(group, own, got, x)


def part(group, out, first, plain, rim):
    _, z, _ = place_in_mode()
    for lower, order in ((True, (rim, plain)), (False, (plain, rim))):
        for shift in range(2):

            @pl.when(((z < 2) == lower) & (first == shift))
            def _():
                split = order[0].shape[1] - shift * group
                out[:, :split] = order[0][:, shift * group :]
                out[:, split:] = order[1][:, : out.shape[1] - split]


def last_kernel(group, at, piece, passed, rim, *refs):
    cross, own = refs[-2:]
    _, z, x = place_in_mode()
    rows = slice(at, at + piece.shape[0])
    inside = (z == 1) | (z == 2)
    for here, plain in ((inside, piece), (jnp.logical_not(inside), passed.at[rows, :])):

        @pl.when(here)
        def _():
            part(group, cross, 1 - x, plain, rim.at[rows, :])
            part(group, own, x, plain, rim.at[rows, :])


def onward_kernel(group, plain, rim, ext, *refs):
    cross, own, passed, far_rim, *inner = refs[-4 - len(PIECES) :]
    _, z, x = place_in_mode()
    part(group, cross, 1 - x, plain, rim)
    part(group, own, x, plain, rim)
    two = 2 * group

    @pl.when(z < 2)
    def _():
        passed[:, :two] = rim[...]
        passed[:, two:] = plain[:, :two]

    @pl.when(z >= 2)
    def _():
        passed[:, :two] = plain[:, two:]
        passed[:, two:] = rim[...]

    target = 3 - z
    cut(group, far_rim, ext, jnp.where(target < 2, 2 * target, 2 * target + 4))
    start = aligned(jnp.where(target < 2, 2 * target + 2, 2 * target), group)
    at = 0
    for out in inner:
        rows, span = out.shape
        out[...] = ext[at : at + rows, pl.ds(start, span)]
        at += rows


def cutting(kernel, shapes, name, *operands, after=()):
    return pl.pallas_call(
        kernel,
        out_shape=[jax.ShapeDtypeStruct(shape, jnp.bfloat16) for shape in shapes],
        in_specs=[VMEM] * len(operands) + [ANY] * len(after),
        out_specs=[VMEM] * len(shapes),
        compiler_params=params(),
        name=name,
    )(*operands, *after)


def fill(lhs, centre, slots, middle):
    _, _, x = place_in_mode()
    width = centre.shape[1] // 2
    for slot, sides in enumerate(slots):
        for side, chunks in enumerate(sides):
            chip = aligned(lax.rem(x + side, 2), width)
            at = 0
            for chunk in chunks:
                first = (2 * slot + side) * width + at
                count = chunk.shape[0]
                lhs[first : first + count, :] = chunk[...]
                centre[slot, pl.ds(pl.multiple_of(chip + at, 16), count), :] = chunk[:, middle]
                at += count


def regroup(layout, refs):
    refs = iter(refs)
    return [[[next(refs) for _ in range(chunks)] for _ in range(2)] for chunks in layout]


def image_kernel(layout, middle, *refs):
    image, centre, lhs = refs[-3:]
    pieces = 2 * sum(layout)
    band = refs[pieces]
    fill(lhs, centre, regroup(layout, refs[:pieces]), middle)
    image[...] = lax.dot_general(
        lhs[...], band[...], NT, preferred_element_type=jnp.float32
    ).astype(jnp.bfloat16)


def flat(slots):
    layout = [len(sides[0]) for sides in slots]
    return layout, [chunk for sides in slots for chunks in sides for chunk in chunks]


def make_image(slots, band, group, width, after):
    layout, pieces = flat(slots)
    span = pieces[0].shape[1]
    return pl.pallas_call(
        functools.partial(image_kernel, layout, slice(2 * group, 3 * group)),
        out_shape=(
            jax.ShapeDtypeStruct((4 * width, band.shape[0]), jnp.bfloat16),
            jax.ShapeDtypeStruct((2, 2 * width, group), jnp.bfloat16),
        ),
        in_specs=[VMEM] * (len(pieces) + 1) + [ANY] * len(after),
        out_specs=(VMEM, VMEM),
        scratch_shapes=[pltpu.VMEM((4 * width, span), jnp.bfloat16)],
        compiler_params=params(),
        cost_estimate=pl.CostEstimate(
            flops=8 * width * span * band.shape[0], bytes_accessed=2**22, transcendentals=0
        ),
        name="image",
    )(*pieces, band, *after)


def project_kernel(matrix, layout, middle, scaling, rows_out, *refs):
    keep, send, own_rows, stacked, late, lhs = refs[-6:]
    band, image, centre = refs[-9:-6]
    _, z, _ = place_in_mode()
    pair = centre.shape[1]
    total, depth = own_rows.shape
    half = total // 2
    chunk = min(rows_out, pair)
    columns = slice(matrix * depth, (matrix + 1) * depth)
    fill(lhs, late, regroup(layout, refs[:-9]), middle)
    stacked[: 2 * pair, :] = image[:, columns]
    stacked[2 * pair :, :] = lax.dot_general(
        lhs[...], band[columns, :], NT, preferred_element_type=jnp.float32
    ).astype(jnp.bfloat16)
    for slot, chip_row in enumerate((z, behind(z), ahead(z), 3 - z)):
        source = (centre, late)[slot // 2]
        for piece in range(pair // chunk):
            first = chip_row * pair + piece * chunk
            target = (
                lax.rem(lax.div(first, rows_out), 2) * half
                + lax.div(first, 2 * rows_out) * rows_out
                + lax.rem(first, rows_out)
            )
            own_rows[pl.ds(pl.multiple_of(target, chunk), chunk), :] = source[
                slot % 2, piece * chunk : (piece + 1) * chunk, :
            ]
    sub = lax.axis_index("sub")
    for out, side in ((send, 1 - sub), (keep, sub)):
        out[...] = (
            lax.dot_general(
                stacked[...],
                own_rows[pl.ds(aligned(side, half), half), :],
                NT,
                preferred_element_type=jnp.float32,
            )
            * scaling
        )


def make_projection(matrix, slots, band, image, centre, group, scaling, rows_out):
    layout, pieces = flat(slots)
    total = 2 * image.shape[0]
    part = jax.ShapeDtypeStruct((total, total // 2), jnp.float32)
    return pl.pallas_call(
        functools.partial(
            project_kernel, matrix, layout, slice(2 * group, 3 * group), scaling, rows_out
        ),
        out_shape=(part, part),
        in_specs=[VMEM] * (len(pieces) + 3),
        out_specs=(VMEM, VMEM),
        scratch_shapes=[
            pltpu.VMEM((total, group), jnp.bfloat16),
            pltpu.VMEM((total, group), jnp.bfloat16),
            pltpu.VMEM(centre.shape, jnp.bfloat16),
            pltpu.VMEM((total // 2, pieces[0].shape[1]), jnp.bfloat16),
        ],
        compiler_params=params(),
        cost_estimate=pl.CostEstimate(
            flops=2 * total * total * group, bytes_accessed=2**21, transcendentals=0
        ),
        name="project",
    )(*pieces, band, image, centre)


def body(modes, gyroscopic, centrifugal, pattern):
    mode_count = lax.axis_size("mode")
    dof_count = lax.axis_size("dof")
    sub_count = lax.axis_size("sub")
    unit_count = dof_count * sub_count
    rows_dev = gyroscopic.shape[1]
    block_size = gyroscopic.shape[3]
    per_unit = rows_dev * mode_count
    block_total = unit_count * per_unit
    group = rows_dev * block_size
    width = modes.shape[1]
    total = width * mode_count

    def move(array, to):
        target, flip = to
        pairs = [(i, target(i // X) * X + (i % X ^ flip)) for i in range(mode_count)]
        return lax.ppermute(array, "mode", pairs)

    def to_ahead(z):
        return 3 * (z + 1) % 5 - 1

    def to_behind(z):
        return 2 * (z + 1) % 5 - 1

    def to_far(z):
        return 3 - z

    def to_near(z):
        return z ^ 1

    def to_inside(z):
        return 3 - z if z in (1, 2) else z

    def to_same(z):
        return z

    phi = modes.T
    forward, backward = ring(unit_count)
    rim = HB * block_size
    plainA = move(cut_plain(phi, group), (to_ahead, 0))
    units = ("dof", "sub")
    if unit_count == 2:
        below = above = lax.ppermute(phi, units, forward)
    else:
        below = lax.ppermute(phi[:, phi.shape[1] - rim :], units, forward)
        above = lax.ppermute(phi[:, :rim], units, backward)

    w5, w6 = 5 * group, 6 * group
    ext, ahead_w, behind_w, cross0_w, own0 = cutting(
        functools.partial(first_kernel, group, rim),
        [(width, w) for w in (phi.shape[1] + 2 * rim, 2 * group, w6, w5, w5)],
        "first",
        stage(phi),
        below,
        above,
    )
    gotA = move(ahead_w, (to_ahead, 0))
    gotB = move(behind_w, (to_behind, 0))
    cross0 = move(cross0_w, (to_same, 1))
    band = make_band(pattern, gyroscopic, centrifugal, own0, w5, per_unit, block_total)

    crossA_w, ownA, passed_w, far_rim_w, *inner_w = cutting(
        functools.partial(onward_kernel, group),
        [(width, w) for w in (w5, w5, 4 * group, 2 * group)]
        + [(rows, 4 * group) for rows in PIECES],
        "onward",
        plainA,
        gotA,
        ext,
        after=(band,),
    )
    far_rim = move(far_rim_w, (to_far, 0))
    passed = move(passed_w, (to_near, 0))
    inner = [move(piece, (to_inside, 0)) for piece in inner_w]
    crossA = move(crossA_w, (to_same, 1))
    crossB_w, ownB = cutting(
        functools.partial(parted_kernel, group),
        [(width, w5), (width, w5)],
        "parted",
        gotB,
        after=(crossA_w,),
    )
    crossB = move(crossB_w, (to_same, 1))
    image, centre = make_image(
        [([own0], [cross0]), ([ownA], [crossA])], band, group, width, (inner[0],)
    )
    ownC, crossC = [], []
    for number, piece in enumerate(inner):
        cross_w, own = cutting(
            functools.partial(last_kernel, group, sum(PIECES[:number])),
            [(piece.shape[0], w5)] * 2,
            "last",
            piece,
            passed,
            far_rim,
            after=(image,),
        )
        ownC.append(own)
        crossC.append(move(cross_w, (to_same, 1)))

    scaling = 1.0 / math.sqrt(block_total * block_size)
    sums = []
    for matrix in range(2):
        keep, send = make_projection(
            matrix,
            [([ownB], [crossB]), (ownC, crossC)],
            band,
            image,
            centre,
            group,
            scaling,
            total // unit_count,
        )
        sums.append(keep + lax.ppermute(send, "sub", [(0, 1), (1, 0)]))
    chip = jnp.stack(sums)
    result = chip[:, :width]
    for slot, to in ((0, to_same), (1, to_behind), (2, to_ahead), (3, to_far)):
        for flip in range(X):
            if slot == 0 and flip == 0:
                continue
            first = (slot * X + flip) * width
            message = chip[:, first : first + width].astype(jnp.bfloat16)
            result = result + move(message, (to, flip)).astype(jnp.float32)
    if dof_count > 1:
        result = lax.psum_scatter(result, "dof", scatter_dimension=2, tiled=True)
    return result.transpose(0, 2, 1)


def solution(mesh):
    return jax.shard_map(
        body,
        mesh=mesh,
        in_specs=(
            P(("dof", "sub"), ("parts", "mode")),
            P(("parts", "dof", "sub"), "mode", None, None, None),
            P(("parts", "dof", "sub"), "mode", None, None, None),
            P(("dof", "sub"), "mode", None),
        ),
        out_specs=P("parts", ("dof", "sub"), "mode"),
        check_vma=False,
    )
```

```python
import functools
import math

import jax
import jax.numpy as jnp
from jax import lax
from jax.experimental import pallas as pl
from jax.experimental.pallas import tpu as pltpu
from jax.sharding import PartitionSpec as P

HB = 8
X = 2
PIECES = (32, 32)
VMEM_LIMIT = 24 * 1024 * 1024
NT = (((1,), (1,)), ((), ()))
VMEM = pl.BlockSpec(memory_space=pltpu.VMEM)
ANY = pl.BlockSpec(memory_space=pl.ANY)


def params():
    return pltpu.CompilerParams(vmem_limit_bytes=VMEM_LIMIT)


def ring(count):
    forward = [(i, (i + 1) % count) for i in range(count)]
    return forward, [(target, source) for source, target in forward]


def place_in_mode():
    m = lax.axis_index("mode")
    return m, lax.div(m, X), lax.rem(m, X)


def ahead(z):
    return lax.rem(3 * (z + 1), 5) - 1


def behind(z):
    return lax.rem(2 * (z + 1), 5) - 1


def aligned(index, size):
    return pl.multiple_of(index * size, size)


def band_kernel(per_unit, block_total, pattern, gyro, spin, _, band):
    row = pl.program_id(0)
    slots, size = gyro.shape[2:4]
    unit = lax.axis_index(("dof", "sub"))
    base = unit * per_unit + lax.axis_index("mode") * pl.num_programs(0) - HB
    band[...] = jnp.zeros_like(band)
    for slot in range(slots):
        column = lax.rem(pattern[0, row, slot] - base + block_total, block_total)
        where = pl.ds(aligned(column, size), size)
        band[0, 0, :, where] = gyro[0, 0, slot]
        band[1, 0, :, where] = spin[0, 0, slot]


def make_band(pattern, gyroscopic, centrifugal, after, width, per_unit, block_total):
    _, rows, slots, size, _ = gyroscopic.shape
    block = pl.BlockSpec((1, 1, slots, size, size), lambda j: (0, j, 0, 0, 0))
    band = pl.pallas_call(
        functools.partial(band_kernel, per_unit, block_total),
        out_shape=jax.ShapeDtypeStruct((2, rows, size, width), jnp.bfloat16),
        grid=(rows,),
        in_specs=[pl.BlockSpec(memory_space=pltpu.SMEM), block, block, ANY],
        out_specs=pl.BlockSpec((2, 1, size, width), lambda j: (0, j, 0, 0)),
        compiler_params=params(),
        cost_estimate=pl.CostEstimate(flops=0, bytes_accessed=2**23, transcendentals=0),
        name="band",
    )(pattern, gyroscopic, centrifugal, after)
    return band.reshape(2 * rows * size, width)


def cut(group, out, source, start):
    out[...] = source[:, pl.ds(aligned(start, group), out.shape[1])]


def plain_start(z):
    return jnp.where(z < 2, 2 * z, 2 * z - 2)


def plain_kernel(group, phi, out):
    _, z, _ = place_in_mode()
    pltpu.sync_copy(phi.at[:, pl.ds(aligned(plain_start(ahead(z)), group), out.shape[1])], out)


def cut_plain(phi, group):
    return pl.pallas_call(
        functools.partial(plain_kernel, group),
        out_shape=jax.ShapeDtypeStruct((phi.shape[0], 4 * group), phi.dtype),
        in_specs=[ANY],
        out_specs=VMEM,
        compiler_params=params(),
        name="plain",
    )(phi)


def stage_kernel(phi, out):
    pltpu.sync_copy(phi, out)


def stage(phi):
    return pl.pallas_call(
        stage_kernel,
        out_shape=jax.ShapeDtypeStruct(phi.shape, phi.dtype),
        in_specs=[ANY],
        out_specs=VMEM,
        compiler_params=params(),
        name="stage",
    )(phi)


def first_kernel(group, rim, phi, below, above, ext, to_ahead, to_behind, cross, own):
    m, z, _ = place_in_mode()
    ext[:, :rim] = below[:, below.shape[1] - rim :]
    ext[:, rim : rim + phi.shape[1]] = phi[...]
    ext[:, rim + phi.shape[1] :] = above[:, :rim]
    target = ahead(z)
    cut(group, to_ahead, ext, jnp.where(target < 2, 2 * target, 2 * target + 4))
    cut(group, to_behind, ext, 2 * behind(z))
    cut(group, cross, ext, m + 1 - 2 * lax.rem(m, 2))
    cut(group, own, ext, m)


def parted_kernel(group, got, *refs):
    cross, own = refs[-2:]
    _, _, x = place_in_mode()
    cut(group, cross, got, 1 - x)
    cut(group, own, got, x)


def part(group, out, first, plain, rim):
    _, z, _ = place_in_mode()
    for lower, order in ((True, (rim, plain)), (False, (plain, rim))):
        for shift in range(2):

            @pl.when(((z < 2) == lower) & (first == shift))
            def _():
                split = order[0].shape[1] - shift * group
                out[:, :split] = order[0][:, shift * group :]
                out[:, split:] = order[1][:, : out.shape[1] - split]


def last_kernel(group, at, piece, passed, rim, *refs):
    cross, own = refs[-2:]
    _, z, x = place_in_mode()
    rows = slice(at, at + piece.shape[0])
    inside = (z == 1) | (z == 2)
    for here, plain in ((inside, piece), (jnp.logical_not(inside), passed.at[rows, :])):

        @pl.when(here)
        def _():
            part(group, cross, 1 - x, plain, rim.at[rows, :])
            part(group, own, x, plain, rim.at[rows, :])


def onward_kernel(group, plain, rim, ext, *refs):
    cross, own, passed, far_rim, *inner = refs[-4 - len(PIECES) :]
    _, z, x = place_in_mode()
    part(group, cross, 1 - x, plain, rim)
    part(group, own, x, plain, rim)
    two = 2 * group

    @pl.when(z < 2)
    def _():
        passed[:, :two] = rim[...]
        passed[:, two:] = plain[:, :two]

    @pl.when(z >= 2)
    def _():
        passed[:, :two] = plain[:, two:]
        passed[:, two:] = rim[...]

    target = 3 - z
    cut(group, far_rim, ext, jnp.where(target < 2, 2 * target, 2 * target + 4))
    start = aligned(jnp.where(target < 2, 2 * target + 2, 2 * target), group)
    at = 0
    for out in inner:
        rows, span = out.shape
        out[...] = ext[at : at + rows, pl.ds(start, span)]
        at += rows


def cutting(kernel, shapes, name, *operands, after=()):
    return pl.pallas_call(
        kernel,
        out_shape=[jax.ShapeDtypeStruct(shape, jnp.bfloat16) for shape in shapes],
        in_specs=[VMEM] * len(operands) + [ANY] * len(after),
        out_specs=[VMEM] * len(shapes),
        compiler_params=params(),
        name=name,
    )(*operands, *after)


def fill(lhs, centre, slots, middle):
    _, _, x = place_in_mode()
    width = centre.shape[1] // 2
    for slot, sides in enumerate(slots):
        for side, chunks in enumerate(sides):
            chip = aligned(lax.rem(x + side, 2), width)
            at = 0
            for chunk in chunks:
                first = (2 * slot + side) * width + at
                count = chunk.shape[0]
                lhs[first : first + count, :] = chunk[...]
                centre[slot, pl.ds(pl.multiple_of(chip + at, 16), count), :] = chunk[:, middle]
                at += count


def regroup(layout, refs):
    refs = iter(refs)
    return [[[next(refs) for _ in range(chunks)] for _ in range(2)] for chunks in layout]


def image_kernel(layout, middle, *refs):
    image, centre, lhs = refs[-3:]
    pieces = 2 * sum(layout)
    band = refs[pieces]
    fill(lhs, centre, regroup(layout, refs[:pieces]), middle)
    image[...] = lax.dot_general(
        lhs[...], band[...], NT, preferred_element_type=jnp.float32
    ).astype(jnp.bfloat16)


def flat(slots):
    layout = [len(sides[0]) for sides in slots]
    return layout, [chunk for sides in slots for chunks in sides for chunk in chunks]


def make_image(slots, band, group, width, after):
    layout, pieces = flat(slots)
    span = pieces[0].shape[1]
    return pl.pallas_call(
        functools.partial(image_kernel, layout, slice(2 * group, 3 * group)),
        out_shape=(
            jax.ShapeDtypeStruct((4 * width, band.shape[0]), jnp.bfloat16),
            jax.ShapeDtypeStruct((2, 2 * width, group), jnp.bfloat16),
        ),
        in_specs=[VMEM] * (len(pieces) + 1) + [ANY] * len(after),
        out_specs=(VMEM, VMEM),
        scratch_shapes=[pltpu.VMEM((4 * width, span), jnp.bfloat16)],
        compiler_params=params(),
        cost_estimate=pl.CostEstimate(
            flops=8 * width * span * band.shape[0], bytes_accessed=2**22, transcendentals=0
        ),
        name="image",
    )(*pieces, band, *after)


def project_kernel(matrix, layout, middle, scaling, rows_out, *refs):
    keep, send, own_rows, stacked, late, lhs = refs[-6:]
    band, image, centre = refs[-9:-6]
    _, z, _ = place_in_mode()
    pair = centre.shape[1]
    total, depth = own_rows.shape
    half = total // 2
    chunk = min(rows_out, pair)
    columns = slice(matrix * depth, (matrix + 1) * depth)
    fill(lhs, late, regroup(layout, refs[:-9]), middle)
    stacked[: 2 * pair, :] = image[:, columns]
    stacked[2 * pair :, :] = lax.dot_general(
        lhs[...], band[columns, :], NT, preferred_element_type=jnp.float32
    ).astype(jnp.bfloat16)
    for slot, chip_row in enumerate((z, behind(z), ahead(z), 3 - z)):
        source = (centre, late)[slot // 2]
        for piece in range(pair // chunk):
            first = chip_row * pair + piece * chunk
            target = (
                lax.rem(lax.div(first, rows_out), 2) * half
                + lax.div(first, 2 * rows_out) * rows_out
                + lax.rem(first, rows_out)
            )
            own_rows[pl.ds(pl.multiple_of(target, chunk), chunk), :] = source[
                slot % 2, piece * chunk : (piece + 1) * chunk, :
            ]
    sub = lax.axis_index("sub")
    for out, side in ((send, 1 - sub), (keep, sub)):
        out[...] = (
            lax.dot_general(
                stacked[...],
                own_rows[pl.ds(aligned(side, half), half), :],
                NT,
                preferred_element_type=jnp.float32,
            )
            * scaling
        )


def make_projection(matrix, slots, band, image, centre, group, scaling, rows_out):
    layout, pieces = flat(slots)
    total = 2 * image.shape[0]
    part = jax.ShapeDtypeStruct((total, total // 2), jnp.float32)
    return pl.pallas_call(
        functools.partial(
            project_kernel, matrix, layout, slice(2 * group, 3 * group), scaling, rows_out
        ),
        out_shape=(part, part),
        in_specs=[VMEM] * (len(pieces) + 3),
        out_specs=(VMEM, VMEM),
        scratch_shapes=[
            pltpu.VMEM((total, group), jnp.bfloat16),
            pltpu.VMEM((total, group), jnp.bfloat16),
            pltpu.VMEM(centre.shape, jnp.bfloat16),
            pltpu.VMEM((total // 2, pieces[0].shape[1]), jnp.bfloat16),
        ],
        compiler_params=params(),
        cost_estimate=pl.CostEstimate(
            flops=2 * total * total * group, bytes_accessed=2**21, transcendentals=0
        ),
        name="project",
    )(*pieces, band, image, centre)


def body(modes, gyroscopic, centrifugal, pattern):
    mode_count = lax.axis_size("mode")
    dof_count = lax.axis_size("dof")
    sub_count = lax.axis_size("sub")
    unit_count = dof_count * sub_count
    rows_dev = gyroscopic.shape[1]
    block_size = gyroscopic.shape[3]
    per_unit = rows_dev * mode_count
    block_total = unit_count * per_unit
    group = rows_dev * block_size
    width = modes.shape[1]
    total = width * mode_count

    def move(array, to):
        target, flip = to
        pairs = [(i, target(i // X) * X + (i % X ^ flip)) for i in range(mode_count)]
        return lax.ppermute(array, "mode", pairs)

    def to_ahead(z):
        return 3 * (z + 1) % 5 - 1

    def to_behind(z):
        return 2 * (z + 1) % 5 - 1

    def to_far(z):
        return 3 - z

    def to_near(z):
        return z ^ 1

    def to_inside(z):
        return 3 - z if z in (1, 2) else z

    def to_same(z):
        return z

    phi = modes.T
    forward, backward = ring(unit_count)
    rim = HB * block_size
    plainA = move(cut_plain(phi, group), (to_ahead, 0))
    units = ("dof", "sub")
    if unit_count == 2:
        below = above = lax.ppermute(phi, units, forward)
    else:
        below = lax.ppermute(phi[:, phi.shape[1] - rim :], units, forward)
        above = lax.ppermute(phi[:, :rim], units, backward)

    w5, w6 = 5 * group, 6 * group
    ext, ahead_w, behind_w, cross0_w, own0 = cutting(
        functools.partial(first_kernel, group, rim),
        [(width, w) for w in (phi.shape[1] + 2 * rim, 2 * group, w6, w5, w5)],
        "first",
        stage(phi),
        below,
        above,
    )
    gotA = move(ahead_w, (to_ahead, 0))
    gotB = move(behind_w, (to_behind, 0))
    cross0 = move(cross0_w, (to_same, 1))
    band = make_band(pattern, gyroscopic, centrifugal, own0, w5, per_unit, block_total)

    crossA_w, ownA, passed_w, far_rim_w, *inner_w = cutting(
        functools.partial(onward_kernel, group),
        [(width, w) for w in (w5, w5, 4 * group, 2 * group)]
        + [(rows, 4 * group) for rows in PIECES],
        "onward",
        plainA,
        gotA,
        ext,
        after=(band,),
    )
    far_rim = move(far_rim_w, (to_far, 0))
    passed = move(passed_w, (to_near, 0))
    inner = [move(piece, (to_inside, 0)) for piece in inner_w]
    crossA = move(crossA_w, (to_same, 1))
    crossB_w, ownB = cutting(
        functools.partial(parted_kernel, group),
        [(width, w5), (width, w5)],
        "parted",
        gotB,
        after=(crossA_w,),
    )
    crossB = move(crossB_w, (to_same, 1))
    image, centre = make_image(
        [([own0], [cross0]), ([ownA], [crossA])], band, group, width, (inner[0],)
    )
    ownC, crossC = [], []
    for number, piece in enumerate(inner):
        cross_w, own = cutting(
            functools.partial(last_kernel, group, sum(PIECES[:number])),
            [(piece.shape[0], w5)] * 2,
            "last",
            piece,
            passed,
            far_rim,
            after=(image,),
        )
        ownC.append(own)
        crossC.append(move(cross_w, (to_same, 1)))

    scaling = 1.0 / math.sqrt(block_total * block_size)
    sums = []
    for matrix in range(2):
        keep, send = make_projection(
            matrix,
            [([ownB], [crossB]), (ownC, crossC)],
            band,
            image,
            centre,
            group,
            scaling,
            total // unit_count,
        )
        sums.append(keep + lax.ppermute(send, "sub", [(0, 1), (1, 0)]))
    chip = jnp.stack(sums)
    result = chip[:, :width]
    for slot, flip, to in (
        (3, 0, to_far),
        (0, 1, to_same),
        (2, 0, to_ahead),
        (2, 1, to_ahead),
        (1, 0, to_behind),
        (1, 1, to_behind),
        (3, 1, to_far),
    ):
        first = (slot * X + flip) * width
        message = chip[:, first : first + width].astype(jnp.bfloat16)
        result = result + move(message, (to, flip)).astype(jnp.float32)
    if dof_count > 1:
        result = lax.psum_scatter(result, "dof", scatter_dimension=2, tiled=True)
    return result.transpose(0, 2, 1)


def solution(mesh):
    return jax.shard_map(
        body,
        mesh=mesh,
        in_specs=(
            P(("dof", "sub"), ("parts", "mode")),
            P(("parts", "dof", "sub"), "mode", None, None, None),
            P(("parts", "dof", "sub"), "mode", None, None, None),
            P(("dof", "sub"), "mode", None),
        ),
        out_specs=P("parts", ("dof", "sub"), "mode"),
        check_vma=False,
    )
```
